512 devices in a mesh: front: 8 (over y), row: 8 (over x, core), col: 8 (over z).
Axes of the slice: x: 4, y: 8, z: 8, core: 2. Of those that a mesh axis runs over, the one named last changes fastest.
Arguments:
- front_cols: bfloat16 [65536, 256], P(('front', 'row'), 'col'), parts along dimension 0, as said below
- contrib: bfloat16 [64, 3072, 1536], P(('front', 'col'), 'row'), parts along dimension 0, as said below
- child_blocks: int32 [32, 24], P('front'), parts along dimension 0, may hold values from 0 to 63, as said below
- child_live: int32 [32], P('front'), parts along dimension 0, may hold values from 12 to 24
- finish: int32 [64], P('front'), parts along dimension 0, may hold values from 0 to 7, as said below
Outputs:
- schur: bfloat16 [65536, 8192], P(('front', 'row'), 'col'), parts along dimension 0
The draws below stay inside these ranges and needn't reach their ends.
There are 8 independent parts, one for each index of `front`. The reference program is written for one: setup_inputs(seed, part) draws one part's arguments, and reference() takes and returns one part's arrays. A program takes and returns all parts, laid end to end along the dimension named above; each array names one. Nothing has to cross between parts.
Inputs may be any that keep to these rules, and one draw needn't show every extreme that they name: `child_blocks`: row c holds distinct front blocks. With L the row sorted increasingly, entry q equals L[(q % 3) * 8 + 2 * (r % 4) + r // 4] where r = q // 3. At most 4 entries of a row lie in any aligned group of 8 consecutive block numbers, and exactly 4 in some group. `finish`: each value appears once. `contrib`: for each child c, the two pieces that finish names for c, left half then right half, form a symmetric positive definite matrix. `front_cols`: its leading 256 rows form a symmetric positive definite matrix.
All inputs are finite; a program needn't handle non-finite values.
Results may differ from the reference program's by a relative error of at most 0.008.
Values may be sent and summed in bfloat16 or wider, within the bound.
A program may use at most 64 MiB of HBM per device.

```python
import jax
import jax.numpy as jnp
from jax import lax

NF = 8192
PANEL = 256
BLK = 128
MCB = 3072
SPREAD = 4
CHILDREN = 4
N_ROW = 8
N_COL = 8


def piece_order(key):
    return jax.random.permutation(jax.random.fold_in(key, 99), N_COL).astype(jnp.int32)


def draw_finish(key, part):
    return piece_order(key)


def draw_front_cols(key, part):
    basis_key, diagonal_key, couple_key = jax.random.split(key, 3)
    basis_matrix = jax.random.normal(basis_key, (PANEL, PANEL), jnp.float32)
    couple = 0.06 * jax.random.normal(couple_key, (NF - PANEL, PANEL), jnp.float32)
    diagonal = jax.random.uniform(diagonal_key, (PANEL,), jnp.float32, 0.5, 1.5)
    corner = jnp.dot(basis_matrix, basis_matrix.T, precision=lax.Precision.HIGHEST) / PANEL + jnp.diag(diagonal)
    return jnp.concatenate([corner, couple], axis=0).astype(jnp.bfloat16)


def draw_contrib(key, part):
    inner_width = MCB // 4
    half_width = MCB // 2

    def one_child(member):
        child_key = jax.random.fold_in(key, member)
        factor_key, diagonal_key = jax.random.split(child_key, 2)
        factor = jax.random.normal(factor_key, (MCB, inner_width), jnp.float32)
        diagonal = jax.random.uniform(diagonal_key, (MCB,), jnp.float32, 0.5, 1.5)
        gram = jnp.dot(factor, factor.T, precision=lax.Precision.HIGHEST) / inner_width + jnp.diag(diagonal)
        return gram.reshape(MCB, 2, half_width).transpose(1, 0, 2)
    blocks_all = jax.vmap(one_child)(jnp.arange(N_COL // 2, dtype=jnp.int32))
    pieces = blocks_all.reshape(N_COL, MCB, half_width)
    return pieces[piece_order(key)].astype(jnp.bfloat16)


def draw_child_blocks(key, part):
    group_count = N_ROW
    per_group = NF // (N_ROW * BLK)
    slot_count = group_count * SPREAD
    block_count = MCB // BLK
    run_length = MCB // (N_ROW * BLK)
    half_rows = N_ROW // 2
    places = jnp.arange(block_count, dtype=jnp.int32)
    device_row = places // run_length
    residue = 2 * (device_row % half_rows) + device_row // half_rows
    source_place = places % run_length * N_ROW + residue

    def one_child(member):
        child_key = jax.random.fold_in(key, member + 7)
        pick_key, order_key, offset_key = jax.random.split(child_key, 3)
        favoured = jax.random.randint(pick_key, (), 0, group_count)
        ranking = jax.random.permutation(order_key, slot_count).astype(jnp.int32)
        slot_ids = jnp.arange(slot_count, dtype=jnp.int32)
        scores = ranking + jnp.where(slot_ids // SPREAD == favoured, -slot_count, 0)
        chosen = jnp.argsort(scores, stable=True)[:block_count].astype(jnp.int32)

        def group_offsets(group_key):
            return jnp.sort(jax.random.permutation(group_key, per_group)[:SPREAD].astype(jnp.int32))
        offsets = jax.vmap(group_offsets)(jax.random.split(offset_key, group_count))
        parent = chosen // SPREAD * per_group + offsets[chosen // SPREAD, chosen % SPREAD]
        ordered = jnp.sort(parent).astype(jnp.int32)
        return ordered[source_place].astype(jnp.int32)
    return jax.vmap(one_child)(jnp.arange(N_COL // 2, dtype=jnp.int32))


def set_ends(entries, rng, smallest, high):
    longest = entries.shape.index(max(entries.shape))
    spots = []
    for shift in (0, 1):
        where = [jax.random.randint(jax.random.fold_in(rng, axis), (), 0, length) for axis, length in enumerate(entries.shape)]
        where[longest] = (where[longest] + shift) % entries.shape[longest]
        spots.append(tuple(where))
    return entries.at[spots[0]].set(smallest).at[spots[1]].set(high)


def setup_inputs(seed: int = 0, part: int = 0) -> dict:
    splits = jax.random.split(jax.random.key(seed), 6)
    own_keys = jax.random.split(jax.random.fold_in(splits[5], part), 6)
    return {
        "front_cols": draw_front_cols(jax.random.fold_in(jax.random.fold_in(splits[5], part), 71), part),
        "contrib": draw_contrib(jax.random.fold_in(jax.random.fold_in(splits[5], part), 71), part),
        "child_blocks": draw_child_blocks(jax.random.fold_in(jax.random.fold_in(splits[5], part), 71), part),
        "child_live": set_ends(jax.random.randint(own_keys[3], (CHILDREN,), MCB // (2 * BLK), MCB // BLK + 1), jax.random.fold_in(own_keys[3], 1), MCB // (2 * BLK), (MCB // BLK + 1) - 1).astype(jnp.int32),
        "finish": draw_finish(jax.random.fold_in(jax.random.fold_in(splits[5], part), 71), part),
    }


def reference(front_cols, contrib, child_blocks, child_live, finish):
    offsets = jnp.arange(BLK, dtype=jnp.int32)
    lane_ids = jnp.arange(MCB, dtype=jnp.int32)
    piece_ids = jnp.arange(N_COL, dtype=jnp.int32)
    order = finish.astype(jnp.int32)
    assembled = jnp.zeros((NF, NF), jnp.float32)
    assembled = assembled.at[:, :PANEL].add(front_cols.astype(jnp.float32))
    for child in range(N_COL // 2):
        left_at = jnp.sum(jnp.where(order == 2 * child, piece_ids, 0)).astype(jnp.int32)
        right_at = jnp.sum(jnp.where(order == 2 * child + 1, piece_ids, 0)).astype(jnp.int32)
        contribution = jnp.concatenate([contrib[left_at], contrib[right_at]], axis=1).astype(jnp.float32)
        live_rows = child_live[child].astype(jnp.int32) * BLK
        keep_mask = (lane_ids[:, None] < live_rows) & (lane_ids[None, :] < live_rows) & (lane_ids[:, None] >= lane_ids[None, :])
        contribution = jnp.where(keep_mask, contribution, 0.0)
        position = (child_blocks[child].astype(jnp.int32)[:, None] * BLK + offsets[None, :]).reshape(-1)
        assembled = assembled.at[position[:, None], position[None, :]].add(contribution)
    row_ids = jnp.arange(NF, dtype=jnp.int32)
    lower_part = row_ids[:, None] >= row_ids[None, :]
    assembled = jnp.where(lower_part, assembled, 0.0)
    corner = assembled[:PANEL, :PANEL]
    corner = corner + jnp.tril(corner, -1).T
    factor = jnp.linalg.cholesky(corner)
    solved = lax.linalg.triangular_solve(factor, assembled[:, :PANEL], left_side=False, lower=True, transpose_a=True)
    update = jnp.dot(solved.astype(jnp.float32), solved.T.astype(jnp.float32), precision=lax.Precision.HIGHEST, preferred_element_type=jnp.float32)
    keep_out = lower_part & (row_ids[:, None] >= PANEL) & (row_ids[None, :] >= PANEL)
    return jnp.where(keep_out, assembled - update, 0.0).astype(jnp.bfloat16)
```

```python
import jax
import jax.numpy as jnp
from jax import lax
from jax.experimental import pallas as pl
from jax.experimental.pallas import tpu as pltpu
from jax.sharding import PartitionSpec as P

BLK = 128
PANEL = 256
N = 8
CHIPS = 4
BLOCKS = 24
BF16 = jnp.bfloat16
F32 = jnp.float32
LAG = 1


def copy_to(src, dst, send, recv, **device):
    return pltpu.make_async_remote_copy(
        src_ref=src,
        dst_ref=dst,
        send_sem=send,
        recv_sem=recv,
        device_id=device,
        device_id_type=pl.DeviceIdType.MESH,
    )


def ring_offset(i):
    return jnp.where(i % 2 == 1, (i + 1) // 2, (N - i // 2) % N)


def first_kept(col):
    return jnp.where(col < 4, 0, jnp.where(col < 6, 1, 2))


def chosen(cases):
    value = cases[0][1]
    for holds, other in cases[1:]:
        value = jnp.where(holds, other, value)
    return value


def column_block(m):
    place = 3 * (m % 4) + m // 4
    return slice(place * BLK, (place + 1) * BLK)


def exchange_kernel(
    cb, live, fin, contrib, fcp,
    xr_o, pr_o, pc_o, co_o,
    px, pxr, pz, pzr, pb, pr, pt, pc, co, zs, zr, xs, xr,
    px_s, px_r, pz_s, pz_r, pr_s, pr_r, t_s, t_r, pc_s, pc_r, co_s, co_r,
    z_s, z_r, x_s, x_r, f_s, f_r, o_s,
):
    row = lax.axis_index("row")
    col = lax.axis_index("col")
    chip = row // 2
    core = row % 2
    mate = 2 * chip + 1 - core

    barrier = pltpu.get_barrier_semaphore()

    @pl.loop(1, N)
    def _(d):
        pl.semaphore_signal(barrier, 1, device_id={"row": (row + d) % N}, device_id_type=pl.DeviceIdType.MESH)
        pl.semaphore_signal(barrier, 1, device_id={"col": (col + d) % N}, device_id_type=pl.DeviceIdType.MESH)

    @pl.when(row != col)
    def _():
        pl.semaphore_signal(barrier, 1, device_id={"row": col, "col": row}, device_id_type=pl.DeviceIdType.MESH)

    piece = fin[col]
    child = piece >> 1
    half = piece & 1
    groups = [cb[child, 3 * row + k] >> 3 for k in range(3)]
    for dest in range(N):
        px[dest] = chosen([(groups[k] == dest, contrib[k, :, 0:BLK]) for k in range(3)])
    pxr[row] = px[row]

    @pl.when(row == col)
    def _():
        pl.semaphore_wait(barrier, 2 * N - 2)

    @pl.when(row != col)
    def _():
        pl.semaphore_wait(barrier, 2 * N - 1)

    def px_copy(dest, slot):
        return copy_to(px.at[dest], pxr.at[slot], px_s.at[dest], px_r.at[slot], row=dest)

    @pl.loop(1, N)
    def _(d):
        dest = (row + d) % N
        px_copy(dest, row).start()

    col_groups = [cb[child, 12 * half + 3 * (m % 4) + m // 4] >> 3 for m in range(12)]
    for dest in range(N):
        first = sum(jnp.where(g < dest, 1, 0) for g in col_groups)
        for k in range(0 if dest < 4 else 1 if dest < 6 else 2, 3):
            for c in range(2):
                ms = range(max(0, 2 * dest - 4 + c), min(2 * dest + 1, 4 * k + 3) + 1)
                zs[dest, k, c] = chosen([(first == m - c, contrib[k, :, column_block(m)]) for m in ms])
    zr[col] = zs[col]

    from_row = [jnp.int32(0)] * N
    for q in range(BLOCKS):
        at = cb[child, q] - N * row
        from_row = [jnp.where(at == b, q // 3, from_row[b]) for b in range(N)]

    @pl.loop(1, N)
    def _(d):
        px_copy((row + d) % N, (row + d) % N).wait_recv()

    for b in range(N):
        pz[b, 0:BLK] = chosen([(from_row[b] == r, pxr[r]) for r in range(N)])
        pz[b, BLK:] = fcp[b]
    pzr[col] = pz[col]

    def pz_copy(dest, slot):
        return copy_to(pz.at[dest], pzr.at[slot], pz_s.at[dest], pz_r.at[slot], col=dest)

    @pl.loop(1, N)
    def _(i):
        dest = (col + ring_offset(i)) % N
        pz_copy(dest, col).start()

    def z_copies(dest, slot, by, act):
        for k in range(3):
            @pl.when(first_kept(by) == k)
            def _():
                act(copy_to(
                    zs.at[dest, pl.ds(k, 3 - k)], zr.at[slot, pl.ds(k, 3 - k)],
                    z_s.at[dest], z_r.at[slot], col=dest,
                ))

    @pl.loop(1, N)
    def _(i):
        dest = (col + ring_offset(i)) % N
        z_copies(dest, col, dest, lambda copy: copy.start())

    @pl.loop(1, N)
    def _(i):
        pz_copy((col + i) % N, (col + i) % N).wait_recv()

    left = jnp.zeros((BLK, BLK), F32)
    right = jnp.zeros((BLK, BLK), F32)
    for j in range(N):
        c = fin[j] >> 1
        column = 12 * (fin[j] & 1)
        q = jnp.int32(-1)
        for a in range(BLOCKS):
            q = jnp.where(cb[c, a] == N * row + col, a, q)
        at = cb[c, column]
        valid = (q >= column) & (q < live[c])
        block = pzr[j, 0:BLK].astype(F32)
        left += jnp.where(valid & (at == 0), block, 0.0)
        right += jnp.where(valid & (at == 1), block, 0.0)
    lane = lax.broadcasted_iota(jnp.int32, (32, BLK), 1) // 32
    packed = [pzr[j, BLK:].astype(F32) for j in range(N)]
    for s in range(4):
        parts = []
        for side in range(2):
            part = jnp.zeros((32, BLK), F32)
            for j in range(4):
                moved = packed[4 * side + j]
                if (j - s) % 4:
                    moved = pltpu.roll(moved, 32 * ((j - s) % 4), 1)
                part = jnp.where(lane == j, moved, part)
            parts.append(part)
        rows = slice(32 * s, 32 * s + 32)
        row_ids = (N * row + col) * BLK + 32 * s + lax.broadcasted_iota(jnp.int32, (32, BLK), 0)
        col_ids = lax.broadcasted_iota(jnp.int32, (32, BLK), 1)
        pb[rows, 0:BLK] = jnp.where(row_ids >= col_ids, left[rows] + parts[0], 0.0).astype(BF16)
        pb[rows, BLK:] = jnp.where(row_ids >= col_ids + BLK, right[rows] + parts[1], 0.0).astype(BF16)
    pr[col] = pb[...]

    def pr_copy(dest, slot):
        return copy_to(pb, pr.at[slot], pr_s.at[dest], pr_r.at[slot], col=dest)

    pt_copy = copy_to(pb, pt, t_s, t_r, row=col, col=row)

    @pl.when(row != col)
    def _():
        pt_copy.start()

    @pl.loop(1, N)
    def _(i):
        dest = (col + ring_offset(i)) % N

        @pl.when((dest <= row) | (row == 0))
        def _():
            pr_copy(dest, col).start()

    @pl.when(row == col)
    def _():
        pt[...] = pb[...]

    @pl.when(row != col)
    def _():
        pt_copy.wait_recv()

    def pc_copy(dest, slot):
        return copy_to(pt, pc.at[slot], pc_s.at[dest], pc_r.at[slot], row=dest)

    @pl.loop(1, N)
    def _(i):
        dest = (row + i) % N

        @pl.when(dest >= col)
        def _():
            pc_copy(dest, row).start()

    pc[row] = pt[...]

    def co_copy(dest):
        return copy_to(pr.at[pl.ds(0, 2)], co, co_s.at[dest], co_r, row=dest)

    @pl.when(row == 0)
    def _():
        for b in range(2):
            @pl.when(col != b)
            def _():
                pr_copy(b, b).wait_recv()

        @pl.loop(1, N)
        def _(dest):
            co_copy(dest).start()

        co[...] = pr[0:2]

    needed = chip >= col // 2

    def x_copy(j, src, dest, slot):
        return copy_to(src, xr.at[core, j, slot], x_s.at[j, dest], x_r.at[j, slot], row=2 * dest + core)

    def f_copy(j, side):
        return copy_to(xr.at[side, j], xr.at[side, j], f_s.at[j], f_r.at[j], row=mate)

    @pl.loop(0, N + LAG)
    def _(i):
        j = (col + ring_offset(i)) % N

        @pl.when(i < N)
        def _():
            @pl.when(i > 0)
            def _():
                z_copies(j, j, col, lambda copy: copy.wait_recv())

            c = fin[j] >> 1
            for dest in range(CHIPS):
                @pl.when(2 * dest + 1 >= col)
                def _():
                    if dest == 0:
                        src = zr.at[j, 0]
                    elif dest == 3:
                        src = zr.at[j, 2]
                    else:
                        src = xs.at[j, dest - 1]
                        later = (cb[c, 3 * row + dest] >> 4) == dest
                        src[...] = jnp.where(later, zr[j, dest], zr[j, dest - 1])

                    @pl.when(chip == dest)
                    def _():
                        xr[core, j, chip] = src[...]

                    @pl.when(chip != dest)
                    def _():
                        x_copy(j, src, dest, chip).start()

        @pl.when((i >= LAG) & needed)
        def _():
            before = (col + ring_offset(i - LAG)) % N
            for slot in range(CHIPS):
                @pl.when(chip != slot)
                def _():
                    x_copy(before, xs.at[before, 0], slot, slot).wait_recv()

            f_copy(before, core).start()

    @pl.when(row != 0)
    def _():
        co_copy(row).wait_recv()

    @pl.loop(1, N)
    def _(i):
        b = (col + i) % N

        @pl.when(((row == 0) & (b > 1)) | ((row > 0) & (col <= row)))
        def _():
            pr_copy(b, b).wait_recv()

        @pl.when(row >= col)
        def _():
            slot = (row + i) % N
            pc_copy(slot, slot).wait_recv()

    out_co = pltpu.make_async_copy(co, co_o, o_s.at[0])
    out_pr = pltpu.make_async_copy(pr, pr_o, o_s.at[1])
    out_pc = pltpu.make_async_copy(pc, pc_o, o_s.at[2])
    out_xr = pltpu.make_async_copy(xr, xr_o, o_s.at[3])
    out_co.start()

    @pl.when(row >= col)
    def _():
        out_pr.start()
        out_pc.start()

    @pl.when(needed)
    def _():
        @pl.loop(0, N)
        def _(j):
            f_copy(j, 1 - core).wait_recv()

    @pl.when(row >= col)
    def _():
        out_xr.start()
        out_xr.wait()
        out_pr.wait()
        out_pc.wait()

    out_co.wait()

    @pl.loop(1, N)
    def _(i):
        r = (row + i) % N
        c = (col + i) % N
        px_copy(r, row).wait_send()
        pz_copy(c, col).wait_send()
        z_copies(c, col, c, lambda copy: copy.wait_send())

        @pl.when((c <= row) | (row == 0))
        def _():
            pr_copy(c, col).wait_send()

        @pl.when(r >= col)
        def _():
            pc_copy(r, row).wait_send()

        @pl.when(row == 0)
        def _():
            co_copy(r).wait_send()

    @pl.when(row != col)
    def _():
        pt_copy.wait_send()

    @pl.loop(0, N)
    def _(j):
        for dest in range(CHIPS):
            @pl.when((2 * dest + 1 >= col) & (chip != dest))
            def _():
                x_copy(j, xs.at[j, 0], dest, chip).wait_send()

        @pl.when(needed)
        def _():
            f_copy(j, core).wait_send()


def exchange(cb, live, fin, contrib, fcp):
    dma = pltpu.SemaphoreType.DMA
    any_ = pl.BlockSpec(memory_space=pl.ANY)
    vmem = pl.BlockSpec(memory_space=pltpu.VMEM)
    smem = pl.BlockSpec(memory_space=pltpu.SMEM)
    block = (BLK, BLK)
    panel = (BLK, PANEL)
    return pl.pallas_call(
        exchange_kernel,
        out_shape=[
            jax.ShapeDtypeStruct((2, N, CHIPS, 2, *block), BF16),
            jax.ShapeDtypeStruct((N, *panel), BF16),
            jax.ShapeDtypeStruct((N, *panel), BF16),
            jax.ShapeDtypeStruct((2, *panel), BF16),
        ],
        in_specs=[smem, smem, smem, vmem, vmem],
        out_specs=[any_] * 4,
        scratch_shapes=[
            pltpu.VMEM((N, *block), BF16),
            pltpu.VMEM((N, *block), BF16),
            pltpu.VMEM((N, BLK + 32, BLK), BF16),
            pltpu.VMEM((N, BLK + 32, BLK), BF16),
            pltpu.VMEM(panel, BF16),
            pltpu.VMEM((N, *panel), BF16),
            pltpu.VMEM(panel, BF16),
            pltpu.VMEM((N, *panel), BF16),
            pltpu.VMEM((2, *panel), BF16),
            pltpu.VMEM((N, 3, 2, *block), BF16),
            pltpu.VMEM((N, 3, 2, *block), BF16),
            pltpu.VMEM((N, 2, 2, *block), BF16),
            pltpu.VMEM((2, N, CHIPS, 2, *block), BF16),
            dma((N,)), dma((N,)),
            dma((N,)), dma((N,)),
            dma((N,)), dma((N,)),
            dma, dma,
            dma((N,)), dma((N,)),
            dma((N,)), dma,
            dma((N,)), dma((N,)),
            dma((N, CHIPS)), dma((N, CHIPS)),
            dma((N,)), dma((N,)),
            dma((4,)),
        ],
        compiler_params=pltpu.CompilerParams(
            collective_id=0, has_side_effects=True, vmem_limit_bytes=40 << 20
        ),
        name="exchange",
    )(cb, live, fin, contrib, fcp)


def dot(a, b):
    return jnp.dot(a, b, preferred_element_type=F32, precision=lax.Precision.HIGHEST)


def small_inverse(d):
    n = d.shape[0]
    rows = lax.broadcasted_iota(jnp.int32, (n, n), 0)
    cols = lax.broadcasted_iota(jnp.int32, (n, n), 1)
    for k in range(n):
        inv = 1.0 / d[k : k + 1, k : k + 1]
        across = d[k : k + 1, :] * inv
        down = d[:, k : k + 1]
        d = d - down * across
        d = jnp.where(rows == k, across, d)
        d = jnp.where(cols == k, jnp.where(rows == k, -inv, down * inv), d)
    return -d


STEP = 32


def sweep_block(a):
    across = a[0:STEP, :]
    down = a[:, 0:STEP]
    inv = small_inverse(a[0:STEP, 0:STEP])
    q = dot(inv, across)
    qt = dot(down, inv)
    a[...] = a[...] - dot(qt, across)
    a[0:STEP, :] = q
    a[:, 0:STEP] = qt
    a[0:STEP, 0:STEP] = -inv
    n = a.shape[0]
    a[...] = pltpu.roll(pltpu.roll(a[...], n - STEP, 0), n - STEP, 1)


def update_kernel(cb, live, fin, xr, pr, pc, co, out, a, t, total, rowq, colq, colc, jof):
    row = lax.axis_index("row")
    col = lax.axis_index("col")
    p = pl.program_id(0)

    @pl.when((p == 0) & (row >= col))
    def _():
        lower = jnp.concatenate([co[0], co[1]], axis=0).astype(F32)
        ri = lax.broadcasted_iota(jnp.int32, (PANEL, PANEL), 0)
        ci = lax.broadcasted_iota(jnp.int32, (PANEL, PANEL), 1)
        a[...] = lower + jnp.where(ri < ci, lower.T, 0.0)

        @pl.loop(0, PANEL // STEP)
        def _(i):
            sweep_block(a)

        m = -a[...]
        high = m.astype(BF16)
        low = (m - high.astype(F32)).astype(BF16)
        rows = pr[...].reshape(N * BLK, PANEL)
        t[...] = (
            jnp.dot(rows, high, preferred_element_type=F32)
            + jnp.dot(rows, low, preferred_element_type=F32)
        ).astype(BF16)

        for i in range(4 * N):
            rowq[i] = -1
            colq[i] = -1
        for j in range(N):
            jof[fin[j]] = j
        for c in range(4):
            for q in range(BLOCKS):
                v = cb[c, q]
                m = 4 * (q % 3) + (q // 3) % 4
                before = q - q % 12 + 3 * ((m - 1) % 4) + (m - 1) // 4

                @pl.when(v >> 3 == row)
                def _():
                    rowq[N * c + (v & 7)] = q

                @pl.when(v >> 3 == col)
                def _():
                    colq[N * c + (v & 7)] = q
                    if m == 0:
                        colc[N * c + (v & 7)] = 0
                    else:
                        colc[N * c + (v & 7)] = jnp.where(cb[c, before] >> 3 == col, 1, 0)

    @pl.when(row < col)
    def _():
        out[...] = jnp.zeros_like(out)

    @pl.when(row >= col)
    def _():
        rows = t[pl.ds(pl.multiple_of(p * BLK, BLK), BLK), :]
        for b in range(0, N, 2):
            columns = pc[b : b + 2].reshape(2 * BLK, PANEL)
            total[:, b * BLK : (b + 2) * BLK] = -lax.dot_general(
                rows, columns, (((1,), (1,)), ((), ())), preferred_element_type=F32
            )
        for c in range(4):
            q = rowq[N * c + p]

            @pl.when((q >= 0) & (q < live[c]))
            def _():
                r = q // 3
                for b in range(N):
                    s = colq[N * c + b]

                    @pl.when((s >= 0) & (s <= q))
                    def _():
                        j = jof[2 * c + jnp.where(s >= 12, 1, 0)]
                        block = xr[r % 2, j, r // 2, colc[N * c + b]]
                        total[:, b * BLK : (b + 1) * BLK] += block.astype(F32)

        ri = (N * row + p) * BLK + lax.broadcasted_iota(jnp.int32, (BLK, N * BLK), 0)
        ci = N * BLK * col + lax.broadcasted_iota(jnp.int32, (BLK, N * BLK), 1)
        keep = (ri >= ci) & (ri >= PANEL) & (ci >= PANEL)
        out[...] = jnp.where(keep, total[...], 0.0).astype(BF16)


def update(cb, live, fin, xr, pr, pc, co):
    smem = pl.BlockSpec(memory_space=pltpu.SMEM)
    vmem = pl.BlockSpec(memory_space=pltpu.VMEM)
    ints = lambda n: pltpu.SMEM((n,), jnp.int32)
    return pl.pallas_call(
        update_kernel,
        grid=(N,),
        out_shape=jax.ShapeDtypeStruct((N * BLK, N * BLK), BF16),
        in_specs=[smem] * 3 + [vmem] * 4,
        out_specs=pl.BlockSpec((BLK, N * BLK), lambda p: (p, 0)),
        scratch_shapes=[
            pltpu.VMEM((PANEL, PANEL), F32),
            pltpu.VMEM((N * BLK, PANEL), BF16),
            pltpu.VMEM((BLK, N * BLK), F32),
            ints(4 * N), ints(4 * N), ints(4 * N), ints(N),
        ],
        compiler_params=pltpu.CompilerParams(vmem_limit_bytes=40 << 20),
        name="update",
    )(cb, live, fin, xr, pr, pc, co)


def body(front_cols, contrib, child_blocks, child_live, finish):
    packed = front_cols.reshape(N, 4, 32, 32).transpose(0, 2, 1, 3).reshape(N, 32, BLK)
    pieces = contrib.reshape(3, BLK, 12 * BLK)
    xr, pr, pc, co = exchange(child_blocks, child_live, finish, pieces, packed)
    return update(child_blocks, child_live, finish, xr, pr, pc, co)


def solution(mesh):
    return jax.shard_map(
        body,
        mesh=mesh,
        in_specs=(
            P(("front", "row"), "col"),
            P(("front", "col"), "row", None),
            P("front", None),
            P("front"),
            P("front"),
        ),
        out_specs=P(("front", "row"), "col"),
        check_vma=False,
    )
```

```python
import jax
import jax.numpy as jnp
from jax import lax
from jax.experimental import pallas as pl
from jax.experimental.pallas import tpu as pltpu
from jax.sharding import PartitionSpec as P

BLK = 128
PANEL = 256
N = 8
CHIPS = 4
BLOCKS = 24
BF16 = jnp.bfloat16
F32 = jnp.float32
LAG = 2
FIRST_BLOCK = 3


def copy_to(src, dst, send, recv, **device):
    return pltpu.make_async_remote_copy(
        src_ref=src,
        dst_ref=dst,
        send_sem=send,
        recv_sem=recv,
        device_id=device,
        device_id_type=pl.DeviceIdType.MESH,
    )


def ring_offset(i):
    return jnp.where(i % 2 == 1, (i + 1) // 2, (N - i // 2) % N)


def first_kept(col):
    return jnp.where(col < 4, 0, jnp.where(col < 6, 1, 2))


def chosen(cases):
    value = cases[0][1]
    for holds, other in cases[1:]:
        value = jnp.where(holds, other, value)
    return value


def column_block(m):
    place = 3 * (m % 4) + m // 4
    return slice(place * BLK, (place + 1) * BLK)


def dot(a, b):
    ah = a.astype(BF16)
    bh = b.astype(BF16)
    al = (a - ah.astype(F32)).astype(BF16)
    bl = (b - bh.astype(F32)).astype(BF16)
    return product(ah, bh) + (product(ah, bl) + product(al, bh))


def product(a, b):
    return jnp.dot(a, b, preferred_element_type=F32)


STEP = 32
TOGETHER = 8


def small_inverse(d):
    n = d.shape[0]
    rows = lax.broadcasted_iota(jnp.int32, (n, n), 0)
    cols = lax.broadcasted_iota(jnp.int32, (n, n), 1)
    for k in range(0, n, TOGETHER):
        down = [jnp.broadcast_to(d[:, k + i : k + i + 1], (n, n)) for i in range(TOGETHER)]
        across = [d[k + i : k + i + 1, :] for i in range(TOGETHER)]
        for p in range(TOGETHER):
            at = k + p
            base = down[p]
            inv = 1.0 / base[at : at + 1, :]
            scales = [base[k + i : k + i + 1, :] * inv for i in range(TOGETHER)]
            scaled = across[p] * inv
            d = d - base * scaled
            for i in range(TOGETHER):
                if i != p:
                    down[i] = jnp.where(rows == at, scales[i], down[i] - base * scales[i])
                    across[i] = across[i] - scales[i] * across[p]
            down[p] = jnp.where(rows == at, -inv, base * inv)
            across[p] = scaled
        for i in range(TOGETHER):
            d = jnp.where(rows == k + i, across[i], d)
        for i in range(TOGETHER):
            d = jnp.where(cols == k + i, down[i], d)
    return -d


def sweep_block(a):
    across = a[0:STEP, :]
    down = a[:, 0:STEP]
    inv = small_inverse(a[0:STEP, 0:STEP])
    q = dot(inv, across)
    qt = dot(down, inv)
    a[...] = a[...] - dot(qt, across)
    a[0:STEP, :] = q
    a[:, 0:STEP] = qt
    a[0:STEP, 0:STEP] = -inv
    n = a.shape[0]
    a[...] = pltpu.roll(pltpu.roll(a[...], n - STEP, 0), n - STEP, 1)


def from_lower(a, co):
    lower = jnp.concatenate([co[0], co[1]], axis=0).astype(F32)
    ri = lax.broadcasted_iota(jnp.int32, (PANEL, PANEL), 0)
    ci = lax.broadcasted_iota(jnp.int32, (PANEL, PANEL), 1)
    a[...] = lower + jnp.where(ri < ci, lower.T, 0.0)


def times_inverse(t, pr, a):
    m = -a[...]
    high = m.astype(BF16)
    low = (m - high.astype(F32)).astype(BF16)
    for b in range(0, N, 2):
        rows = pr[b : b + 2].reshape(2 * BLK, PANEL)
        both = product(rows, high) + product(rows, low)
        t[b : b + 2] = both.astype(BF16).reshape(2, BLK, PANEL)


def exchange_kernel(
    cb, live, fin, contrib, fcp,
    xr_o, t_o, pc_o,
    a, t, px, pxr, pz, pzr, pb, pr, pt, pc, co, zs, zr, xs, xr,
    px_s, px_r, pz_s, pz_r, pr_s, pr_r, t_s, t_r, pc_s, pc_r, co_s, co_r,
    z_s, z_r, x_s, x_r, f_s, f_r, o_s,
):
    row = lax.axis_index("row")
    col = lax.axis_index("col")
    chip = row // 2
    core = row % 2
    mate = 2 * chip + 1 - core

    barrier = pltpu.get_barrier_semaphore()

    @pl.loop(1, N)
    def _(d):
        pl.semaphore_signal(barrier, 1, device_id={"row": (row + d) % N}, device_id_type=pl.DeviceIdType.MESH)
        pl.semaphore_signal(barrier, 1, device_id={"col": (col + d) % N}, device_id_type=pl.DeviceIdType.MESH)

    @pl.when(row != col)
    def _():
        pl.semaphore_signal(barrier, 1, device_id={"row": col, "col": row}, device_id_type=pl.DeviceIdType.MESH)

    piece = fin[col]
    child = piece >> 1
    half = piece & 1
    groups = [cb[child, 3 * row + k] >> 3 for k in range(3)]
    for dest in range(N):
        px[dest] = chosen([(groups[k] == dest, contrib[k, :, 0:BLK]) for k in range(3)])
    pxr[row] = px[row]

    @pl.when(row == col)
    def _():
        pl.semaphore_wait(barrier, 2 * N - 2)

    @pl.when(row != col)
    def _():
        pl.semaphore_wait(barrier, 2 * N - 1)

    def px_copy(dest, slot):
        return copy_to(px.at[dest], pxr.at[slot], px_s.at[dest], px_r.at[slot], row=dest)

    @pl.loop(1, N)
    def _(d):
        dest = (row + d) % N
        px_copy(dest, row).start()

    col_groups = [cb[child, 12 * half + 3 * (m % 4) + m // 4] >> 3 for m in range(12)]
    for dest in range(N):
        first = sum(jnp.where(g < dest, 1, 0) for g in col_groups)
        for k in range(0 if dest < 4 else 1 if dest < 6 else 2, 3):
            for c in range(2):
                ms = range(max(0, 2 * dest - 4 + c), min(2 * dest + 1, 4 * k + 3) + 1)
                zs[dest, k, c] = chosen([(first == m - c, contrib[k, :, column_block(m)]) for m in ms])
    zr[col] = zs[col]

    from_row = [jnp.int32(0)] * N
    for q in range(BLOCKS):
        at = cb[child, q] - N * row
        from_row = [jnp.where(at == b, q // 3, from_row[b]) for b in range(N)]

    @pl.loop(1, N)
    def _(d):
        px_copy((row + d) % N, (row + d) % N).wait_recv()

    for b in range(N):
        pz[b, 0:BLK] = chosen([(from_row[b] == r, pxr[r]) for r in range(N)])
        pz[b, BLK:] = fcp[b]
    pzr[col] = pz[col]

    def pz_copy(dest, slot):
        return copy_to(pz.at[dest], pzr.at[slot], pz_s.at[dest], pz_r.at[slot], col=dest)

    @pl.loop(0, N)
    def _(i):
        dest = jnp.where(row == 0, i, (col + ring_offset(i)) % N)

        @pl.when(dest != col)
        def _():
            pz_copy(dest, col).start()

    def z_copies(dest, slot, by, act):
        for k in range(3):
            @pl.when(first_kept(by) == k)
            def _():
                act(copy_to(
                    zs.at[dest, pl.ds(k, 3 - k)], zr.at[slot, pl.ds(k, 3 - k)],
                    z_s.at[dest], z_r.at[slot], col=dest,
                ))

    def start_z():
        @pl.loop(1, N)
        def _(i):
            dest = (col + ring_offset(i)) % N
            z_copies(dest, col, dest, lambda copy: copy.start())

    @pl.when(chip > 0)
    def _():
        start_z()

    @pl.loop(1, N)
    def _(i):
        pz_copy((col + i) % N, (col + i) % N).wait_recv()

    left = jnp.zeros((BLK, BLK), F32)
    right = jnp.zeros((BLK, BLK), F32)
    for j in range(N):
        c = fin[j] >> 1
        column = 12 * (fin[j] & 1)
        q = jnp.int32(-1)
        for entry in range(BLOCKS):
            q = jnp.where(cb[c, entry] == N * row + col, entry, q)
        at = cb[c, column]
        valid = (q >= column) & (q < live[c])
        block = pzr[j, 0:BLK].astype(F32)
        left += jnp.where(valid & (at == 0), block, 0.0)
        right += jnp.where(valid & (at == 1), block, 0.0)
    lane = lax.broadcasted_iota(jnp.int32, (32, BLK), 1) // 32
    packed = [pzr[j, BLK:].astype(F32) for j in range(N)]
    for s in range(4):
        parts = []
        for side in range(2):
            part = jnp.zeros((32, BLK), F32)
            for j in range(4):
                moved = packed[4 * side + j]
                if (j - s) % 4:
                    moved = pltpu.roll(moved, 32 * ((j - s) % 4), 1)
                part = jnp.where(lane == j, moved, part)
            parts.append(part)
        rows = slice(32 * s, 32 * s + 32)
        row_ids = (N * row + col) * BLK + 32 * s + lax.broadcasted_iota(jnp.int32, (32, BLK), 0)
        col_ids = lax.broadcasted_iota(jnp.int32, (32, BLK), 1)
        pb[rows, 0:BLK] = jnp.where(row_ids >= col_ids, left[rows] + parts[0], 0.0).astype(BF16)
        pb[rows, BLK:] = jnp.where(row_ids >= col_ids + BLK, right[rows] + parts[1], 0.0).astype(BF16)
    pr[col] = pb[...]

    def pr_copy(dest, slot):
        return copy_to(pb, pr.at[slot], pr_s.at[dest], pr_r.at[slot], col=dest)

    pt_copy = copy_to(pb, pt, t_s, t_r, row=col, col=row)

    def co_copy(dest):
        return copy_to(pr.at[pl.ds(0, 2)], co, co_s.at[dest], co_r, row=dest)

    @pl.loop(1, N)
    def _(i):
        dest = (col + ring_offset(i)) % N

        @pl.when((dest <= row) | ((row == 0) & (col < 2)))
        def _():
            pr_copy(dest, col).start()

    @pl.when(row == 0)
    def _():
        for b in range(2):
            @pl.when(col != b)
            def _():
                pr_copy(b, b).wait_recv()

        @pl.loop(1, N)
        def _(dest):
            co_copy(dest).start()

        co[...] = pr[0:2]

    @pl.when(chip == 0)
    def _():
        start_z()

    @pl.when(row != col)
    def _():
        pt_copy.start()

    @pl.when(row == col)
    def _():
        pt[...] = pb[...]

    def pc_copy(dest, slot):
        return copy_to(pt, pc.at[slot], pc_s.at[dest], pc_r.at[slot], row=dest)

    def pass_on_columns():
        @pl.when(row != col)
        def _():
            pt_copy.wait_recv()

        @pl.loop(1, N)
        def _(i):
            dest = (row + i) % N

            @pl.when(dest >= col)
            def _():
                pc_copy(dest, row).start()

        pc[row] = pt[...]

    needed = chip >= col // 2

    def x_copy(j, src, dest, slot):
        return copy_to(src, xr.at[core, j, slot], x_s.at[j, dest], x_r.at[j, slot], row=2 * dest + core)

    def f_copy(j, side):
        return copy_to(xr.at[side, j], xr.at[side, j], f_s.at[j], f_r.at[j], row=mate)

    @pl.loop(0, N + LAG)
    def _(i):
        j = (col + ring_offset(i)) % N

        @pl.when(i < N)
        def _():
            @pl.when(i > 0)
            def _():
                z_copies(j, j, col, lambda copy: copy.wait_recv())

            c = fin[j] >> 1
            for dest in range(CHIPS):
                @pl.when(2 * dest + 1 >= col)
                def _():
                    if dest == 0:
                        src = zr.at[j, 0]
                    elif dest == 3:
                        src = zr.at[j, 2]
                    else:
                        src = xs.at[j, dest - 1]
                        later = (cb[c, 3 * row + dest] >> 4) == dest
                        src[...] = jnp.where(later, zr[j, dest], zr[j, dest - 1])

                    @pl.when(chip == dest)
                    def _():
                        xr[core, j, chip] = src[...]

                    @pl.when(chip != dest)
                    def _():
                        x_copy(j, src, dest, chip).start()

        @pl.when((i >= LAG) & needed)
        def _():
            before = (col + ring_offset(i - LAG)) % N
            for slot in range(CHIPS):
                @pl.when(chip != slot)
                def _():
                    x_copy(before, xs.at[before, 0], slot, slot).wait_recv()

            f_copy(before, core).start()

        @pl.when(i == FIRST_BLOCK)
        def _():
            @pl.when(row != 0)
            def _():
                co_copy(row).wait_recv()

            from_lower(a, co)

        @pl.when((i >= FIRST_BLOCK) & (i < FIRST_BLOCK + 4) & (row >= col))
        def _():
            @pl.loop(0, 2)
            def _(_i):
                sweep_block(a)

    pass_on_columns()

    @pl.when(row >= col)
    def _():
        @pl.loop(1, N)
        def _(i):
            b = (col + i) % N

            @pl.when((row > 0) | (b > 1))
            def _():
                pr_copy(b, b).wait_recv()

    out_t = pltpu.make_async_copy(t, t_o, o_s.at[0])
    out_pc = pltpu.make_async_copy(pc, pc_o, o_s.at[1])
    out_xr = pltpu.make_async_copy(xr, xr_o, o_s.at[2])

    @pl.when(row >= col)
    def _():
        times_inverse(t, pr, a)
        out_t.start()

        @pl.loop(1, N)
        def _(i):
            slot = (row + i) % N
            pc_copy(slot, slot).wait_recv()

        out_pc.start()

    @pl.when(needed)
    def _():
        @pl.loop(0, N)
        def _(j):
            f_copy(j, 1 - core).wait_recv()

    @pl.when(row >= col)
    def _():
        out_xr.start()
        out_xr.wait()
        out_t.wait()
        out_pc.wait()

    @pl.loop(1, N)
    def _(i):
        r = (row + i) % N
        c = (col + i) % N
        px_copy(r, row).wait_send()
        pz_copy(c, col).wait_send()
        z_copies(c, col, c, lambda copy: copy.wait_send())

        @pl.when((c <= row) | ((row == 0) & (col < 2)))
        def _():
            pr_copy(c, col).wait_send()

        @pl.when(r >= col)
        def _():
            pc_copy(r, row).wait_send()

        @pl.when(row == 0)
        def _():
            co_copy(r).wait_send()

    @pl.when(row != col)
    def _():
        pt_copy.wait_send()

    @pl.loop(0, N)
    def _(j):
        for dest in range(CHIPS):
            @pl.when((2 * dest + 1 >= col) & (chip != dest))
            def _():
                x_copy(j, xs.at[j, 0], dest, chip).wait_send()

        @pl.when(needed)
        def _():
            f_copy(j, core).wait_send()


def exchange(cb, live, fin, contrib, fcp):
    dma = pltpu.SemaphoreType.DMA
    any_ = pl.BlockSpec(memory_space=pl.ANY)
    vmem = pl.BlockSpec(memory_space=pltpu.VMEM)
    smem = pl.BlockSpec(memory_space=pltpu.SMEM)
    block = (BLK, BLK)
    panel = (BLK, PANEL)
    return pl.pallas_call(
        exchange_kernel,
        out_shape=[
            jax.ShapeDtypeStruct((2, N, CHIPS, 2, *block), BF16),
            jax.ShapeDtypeStruct((N, *panel), BF16),
            jax.ShapeDtypeStruct((N, *panel), BF16),
        ],
        in_specs=[smem, smem, smem, vmem, vmem],
        out_specs=[any_] * 3,
        scratch_shapes=[
            pltpu.VMEM((PANEL, PANEL), F32),
            pltpu.VMEM((N, *panel), BF16),
            pltpu.VMEM((N, *block), BF16),
            pltpu.VMEM((N, *block), BF16),
            pltpu.VMEM((N, BLK + 32, BLK), BF16),
            pltpu.VMEM((N, BLK + 32, BLK), BF16),
            pltpu.VMEM(panel, BF16),
            pltpu.VMEM((N, *panel), BF16),
            pltpu.VMEM(panel, BF16),
            pltpu.VMEM((N, *panel), BF16),
            pltpu.VMEM((2, *panel), BF16),
            pltpu.VMEM((N, 3, 2, *block), BF16),
            pltpu.VMEM((N, 3, 2, *block), BF16),
            pltpu.VMEM((N, 2, 2, *block), BF16),
            pltpu.VMEM((2, N, CHIPS, 2, *block), BF16),
            dma((N,)), dma((N,)),
            dma((N,)), dma((N,)),
            dma((N,)), dma((N,)),
            dma, dma,
            dma((N,)), dma((N,)),
            dma((N,)), dma,
            dma((N,)), dma((N,)),
            dma((N, CHIPS)), dma((N, CHIPS)),
            dma((N,)), dma((N,)),
            dma((3,)),
        ],
        compiler_params=pltpu.CompilerParams(
            collective_id=0, has_side_effects=True, vmem_limit_bytes=40 << 20
        ),
        name="exchange",
    )(cb, live, fin, contrib, fcp)


def update_kernel(cb, live, fin, xr, t, pc, out, total, rowq, colq, colc, jof):
    row = lax.axis_index("row")
    col = lax.axis_index("col")
    p = pl.program_id(0)

    @pl.when((p == 0) & (row >= col))
    def _():
        for i in range(4 * N):
            rowq[i] = -1
            colq[i] = -1
        for j in range(N):
            jof[fin[j]] = j
        for c in range(4):
            for q in range(BLOCKS):
                v = cb[c, q]
                m = 4 * (q % 3) + (q // 3) % 4
                before = q - q % 12 + 3 * ((m - 1) % 4) + (m - 1) // 4

                @pl.when(v >> 3 == row)
                def _():
                    rowq[N * c + (v & 7)] = q

                @pl.when(v >> 3 == col)
                def _():
                    colq[N * c + (v & 7)] = q
                    if m == 0:
                        colc[N * c + (v & 7)] = 0
                    else:
                        colc[N * c + (v & 7)] = jnp.where(cb[c, before] >> 3 == col, 1, 0)

    @pl.when(row < col)
    def _():
        out[...] = jnp.zeros_like(out)

    @pl.when(row >= col)
    def _():
        rows = t[p]
        for b in range(0, N, 2):
            columns = pc[b : b + 2].reshape(2 * BLK, PANEL)
            total[:, b * BLK : (b + 2) * BLK] = -lax.dot_general(
                rows, columns, (((1,), (1,)), ((), ())), preferred_element_type=F32
            )
        for c in range(4):
            q = rowq[N * c + p]

            @pl.when((q >= 0) & (q < live[c]))
            def _():
                r = q // 3
                for b in range(N):
                    s = colq[N * c + b]

                    @pl.when((s >= 0) & (s <= q))
                    def _():
                        j = jof[2 * c + jnp.where(s >= 12, 1, 0)]
                        block = xr[r % 2, j, r // 2, colc[N * c + b]]
                        total[:, b * BLK : (b + 1) * BLK] += block.astype(F32)

        ri = (N * row + p) * BLK + lax.broadcasted_iota(jnp.int32, (BLK, N * BLK), 0)
        ci = N * BLK * col + lax.broadcasted_iota(jnp.int32, (BLK, N * BLK), 1)
        keep = (ri >= ci) & (ri >= PANEL) & (ci >= PANEL)
        out[...] = jnp.where(keep, total[...], 0.0).astype(BF16)


def update(cb, live, fin, xr, t, pc):
    smem = pl.BlockSpec(memory_space=pltpu.SMEM)
    vmem = pl.BlockSpec(memory_space=pltpu.VMEM)
    ints = lambda n: pltpu.SMEM((n,), jnp.int32)
    return pl.pallas_call(
        update_kernel,
        grid=(N,),
        out_shape=jax.ShapeDtypeStruct((N * BLK, N * BLK), BF16),
        in_specs=[smem] * 3 + [vmem] * 3,
        out_specs=pl.BlockSpec((BLK, N * BLK), lambda p: (p, 0)),
        scratch_shapes=[
            pltpu.VMEM((BLK, N * BLK), F32),
            ints(4 * N), ints(4 * N), ints(4 * N), ints(N),
        ],
        compiler_params=pltpu.CompilerParams(vmem_limit_bytes=40 << 20),
        name="update",
    )(cb, live, fin, xr, t, pc)


def body(front_cols, contrib, child_blocks, child_live, finish):
    packed = front_cols.reshape(N, 4, 32, 32).transpose(0, 2, 1, 3).reshape(N, 32, BLK)
    pieces = contrib.reshape(3, BLK, 12 * BLK)
    xr, t, pc = exchange(child_blocks, child_live, finish, pieces, packed)
    return update(child_blocks, child_live, finish, xr, t, pc)


def solution(mesh):
    return jax.shard_map(
        body,
        mesh=mesh,
        in_specs=(
            P(("front", "row"), "col"),
            P(("front", "col"), "row", None),
            P("front", None),
            P("front"),
            P("front"),
        ),
        out_specs=P(("front", "row"), "col"),
        check_vma=False,
    )
```

```python
import jax
import jax.numpy as jnp
from jax import lax
from jax.experimental import pallas as pl
from jax.experimental.pallas import tpu as pltpu
from jax.sharding import PartitionSpec as P

BLK = 128
PANEL = 256
N = 8
CHIPS = 4
BLOCKS = 24
BF16 = jnp.bfloat16
F32 = jnp.float32
LAG = 2
AHEAD = 2
SUM_STEP = 2
COLUMNS_STEP = 4
FIRST_BLOCK = 4


def copy_to(src, dst, send, recv, **device):
    return pltpu.make_async_remote_copy(
        src_ref=src,
        dst_ref=dst,
        send_sem=send,
        recv_sem=recv,
        device_id=device,
        device_id_type=pl.DeviceIdType.MESH,
    )


def ring_offset(i):
    return jnp.where(i % 2 == 1, (i + 1) // 2, (N - i // 2) % N)


def first_kept(row, col):
    return jnp.maximum(col - 1 - (row % 4) // 2, 0) // 2


def chosen(cases):
    value = cases[0][1]
    for holds, other in cases[1:]:
        value = jnp.where(holds, other, value)
    return value


def column_block(m):
    place = 3 * (m % 4) + m // 4
    return slice(place * BLK, (place + 1) * BLK)


def dot(a, b):
    ah = a.astype(BF16)
    bh = b.astype(BF16)
    al = (a - ah.astype(F32)).astype(BF16)
    bl = (b - bh.astype(F32)).astype(BF16)
    return product(ah, bh) + (product(ah, bl) + product(al, bh))


def product(a, b):
    return jnp.dot(a, b, preferred_element_type=F32)


STEP = 32
TOGETHER = 8


def small_inverse(d):
    n = d.shape[0]
    rows = lax.broadcasted_iota(jnp.int32, (n, n), 0)
    cols = lax.broadcasted_iota(jnp.int32, (n, n), 1)
    for k in range(0, n, TOGETHER):
        down = [jnp.broadcast_to(d[:, k + i : k + i + 1], (n, n)) for i in range(TOGETHER)]
        across = [d[k + i : k + i + 1, :] for i in range(TOGETHER)]
        for p in range(TOGETHER):
            at = k + p
            base = down[p]
            inv = 1.0 / base[at : at + 1, :]
            scales = [base[k + i : k + i + 1, :] * inv for i in range(TOGETHER)]
            scaled = across[p] * inv
            d = d - base * scaled
            for i in range(TOGETHER):
                if i != p:
                    down[i] = jnp.where(rows == at, scales[i], down[i] - base * scales[i])
                    across[i] = across[i] - scales[i] * across[p]
            down[p] = jnp.where(rows == at, -inv, base * inv)
            across[p] = scaled
        for i in range(TOGETHER):
            d = jnp.where(rows == k + i, across[i], d)
        for i in range(TOGETHER):
            d = jnp.where(cols == k + i, down[i], d)
    return -d


def sweep_block(a):
    across = a[0:STEP, :]
    down = a[:, 0:STEP]
    inv = small_inverse(a[0:STEP, 0:STEP])
    q = dot(inv, across)
    qt = dot(down, inv)
    a[...] = a[...] - dot(qt, across)
    a[0:STEP, :] = q
    a[:, 0:STEP] = qt
    a[0:STEP, 0:STEP] = -inv
    n = a.shape[0]
    a[...] = pltpu.roll(pltpu.roll(a[...], n - STEP, 0), n - STEP, 1)


def from_lower(a, co):
    lower = jnp.concatenate([co[0], co[1]], axis=0).astype(F32)
    ri = lax.broadcasted_iota(jnp.int32, (PANEL, PANEL), 0)
    ci = lax.broadcasted_iota(jnp.int32, (PANEL, PANEL), 1)
    a[...] = lower + jnp.where(ri < ci, lower.T, 0.0)


def times_inverse(t, pr, a):
    m = -a[...]
    high = m.astype(BF16)
    low = (m - high.astype(F32)).astype(BF16)
    for b in range(0, N, 2):
        rows = pr[b : b + 2].reshape(2 * BLK, PANEL)
        both = product(rows, high) + product(rows, low)
        t[b : b + 2] = both.astype(BF16).reshape(2, BLK, PANEL)


def exchange_kernel(
    cb, live, fin, contrib, fcp,
    xr_o, t_o, pc_o,
    a, t, px, pxr, pz, pzr, pb, pr, pt, pc, co, zs, zr, xs, xr,
    px_s, px_r, pz_s, pz_r, pr_s, pr_r, t_s, t_r, pc_s, pc_r, co_s, co_r,
    z_s, z_r, x_s, x_r, f_s, f_r, o_s,
):
    row = lax.axis_index("row")
    col = lax.axis_index("col")
    chip = row // 2
    core = row % 2
    mate = 2 * chip + 1 - core

    barrier = pltpu.get_barrier_semaphore()

    @pl.loop(1, N)
    def _(d):
        pl.semaphore_signal(barrier, 1, device_id={"row": (row + d) % N}, device_id_type=pl.DeviceIdType.MESH)
        pl.semaphore_signal(barrier, 1, device_id={"col": (col + d) % N}, device_id_type=pl.DeviceIdType.MESH)

    @pl.when(row != col)
    def _():
        pl.semaphore_signal(barrier, 1, device_id={"row": col, "col": row}, device_id_type=pl.DeviceIdType.MESH)

    piece = fin[col]
    child = piece >> 1
    half = piece & 1
    groups = [cb[child, 3 * row + k] >> 3 for k in range(3)]
    for dest in range(N):
        px[dest] = chosen([(groups[k] == dest, contrib[k, :, 0:BLK]) for k in range(3)])
    pxr[row] = px[row]

    @pl.when(row == col)
    def _():
        pl.semaphore_wait(barrier, 2 * N - 2)

    @pl.when(row != col)
    def _():
        pl.semaphore_wait(barrier, 2 * N - 1)

    def px_copy(dest, slot):
        return copy_to(px.at[dest], pxr.at[slot], px_s.at[dest], px_r.at[slot], row=dest)

    @pl.loop(1, N)
    def _(d):
        dest = (row + d) % N
        px_copy(dest, row).start()

    col_groups = [cb[child, 12 * half + 3 * (m % 4) + m // 4] >> 3 for m in range(12)]
    for dest in range(N):
        first = sum(jnp.where(g < dest, 1, 0) for g in col_groups)
        for k in range(0 if dest < 4 else 1 if dest < 6 else 2, 3):
            for c in range(2):
                ms = range(max(0, 2 * dest - 4 + c), min(2 * dest + 1, 4 * k + 3) + 1)
                zs[dest, k, c] = chosen([(first == m - c, contrib[k, :, column_block(m)]) for m in ms])
    zr[col] = zs[col]

    def z_copies(dest, slot, by, act):
        for k in range(3):
            @pl.when(first_kept(row, by) == k)
            def _():
                act(copy_to(
                    zs.at[dest, pl.ds(k, 3 - k)], zr.at[slot, pl.ds(k, 3 - k)],
                    z_s.at[dest], z_r.at[slot], col=dest,
                ))

    def start_z(first, end):
        @pl.loop(first, end)
        def _(i):
            dest = (col + ring_offset(i)) % N
            z_copies(dest, col, dest, lambda copy: copy.start())

    start_z(1, 1 + AHEAD)

    from_row = [jnp.int32(0)] * N
    for q in range(BLOCKS):
        at = cb[child, q] - N * row
        from_row = [jnp.where(at == b, q // 3, from_row[b]) for b in range(N)]

    @pl.loop(1, N)
    def _(d):
        px_copy((row + d) % N, (row + d) % N).wait_recv()

    for b in range(N):
        pz[b, 0:BLK] = chosen([(from_row[b] == r, pxr[r]) for r in range(N)])
        pz[b, BLK:] = fcp[b]
    pzr[col] = pz[col]

    def pz_copy(dest, slot):
        return copy_to(pz.at[dest], pzr.at[slot], pz_s.at[dest], pz_r.at[slot], col=dest)

    @pl.loop(0, N)
    def _(i):
        dest = jnp.where(row == 0, i, (col + ring_offset(i)) % N)

        @pl.when(dest != col)
        def _():
            pz_copy(dest, col).start()

    def pr_copy(dest, slot):
        return copy_to(pb, pr.at[slot], pr_s.at[dest], pr_r.at[slot], col=dest)

    pt_copy = copy_to(pb, pt, t_s, t_r, row=col, col=row)

    def co_copy(dest):
        return copy_to(pr.at[pl.ds(0, 2)], co, co_s.at[dest], co_r, row=dest)

    def sum_panel():
        @pl.loop(1, N)
        def _(i):
            pz_copy((col + i) % N, (col + i) % N).wait_recv()

        left = jnp.zeros((BLK, BLK), F32)
        right = jnp.zeros((BLK, BLK), F32)
        for j in range(N):
            c = fin[j] >> 1
            column = 12 * (fin[j] & 1)
            q = jnp.int32(-1)
            for entry in range(BLOCKS):
                q = jnp.where(cb[c, entry] == N * row + col, entry, q)
            at = cb[c, column]
            valid = (q >= column) & (q < live[c])
            block = pzr[j, 0:BLK].astype(F32)
            left += jnp.where(valid & (at == 0), block, 0.0)
            right += jnp.where(valid & (at == 1), block, 0.0)
        lane = lax.broadcasted_iota(jnp.int32, (32, BLK), 1) // 32
        packed = [pzr[j, BLK:].astype(F32) for j in range(N)]
        for s in range(4):
            parts = []
            for side in range(2):
                part = jnp.zeros((32, BLK), F32)
                for j in range(4):
                    moved = packed[4 * side + j]
                    if (j - s) % 4:
                        moved = pltpu.roll(moved, 32 * ((j - s) % 4), 1)
                    part = jnp.where(lane == j, moved, part)
                parts.append(part)
            rows = slice(32 * s, 32 * s + 32)
            row_ids = (N * row + col) * BLK + 32 * s + lax.broadcasted_iota(jnp.int32, (32, BLK), 0)
            col_ids = lax.broadcasted_iota(jnp.int32, (32, BLK), 1)
            pb[rows, 0:BLK] = jnp.where(row_ids >= col_ids, left[rows] + parts[0], 0.0).astype(BF16)
            pb[rows, BLK:] = jnp.where(row_ids >= col_ids + BLK, right[rows] + parts[1], 0.0).astype(BF16)
        pr[col] = pb[...]

        @pl.loop(1, N)
        def _(i):
            dest = (col + ring_offset(i)) % N

            @pl.when((dest <= row) | ((row == 0) & (col < 2)))
            def _():
                pr_copy(dest, col).start()

        @pl.when(row == 0)
        def _():
            for b in range(2):
                @pl.when(col != b)
                def _():
                    pr_copy(b, b).wait_recv()

            @pl.loop(1, N)
            def _(dest):
                co_copy(dest).start()

            co[...] = pr[0:2]

        @pl.when(row != col)
        def _():
            pt_copy.start()

        @pl.when(row == col)
        def _():
            pt[...] = pb[...]

    def pc_copy(dest, slot):
        return copy_to(pt, pc.at[slot], pc_s.at[dest], pc_r.at[slot], row=dest)

    def pass_on_columns():
        @pl.when(row != col)
        def _():
            pt_copy.wait_recv()

        @pl.loop(1, N)
        def _(i):
            dest = (row + i) % N

            @pl.when(dest >= col)
            def _():
                pc_copy(dest, row).start()

        pc[row] = pt[...]

    needed = chip >= col // 2

    def x_copy(j, src, dest, slot):
        return copy_to(src, xr.at[core, j, slot], x_s.at[j, dest], x_r.at[j, slot], row=2 * dest + core)

    def f_copy(j, side):
        return copy_to(xr.at[side, j], xr.at[side, j], f_s.at[j], f_r.at[j], row=mate)

    @pl.loop(0, N + LAG)
    def _(i):
        j = (col + ring_offset(i)) % N

        @pl.when(i < N)
        def _():
            @pl.when(i > 0)
            def _():
                z_copies(j, j, col, lambda copy: copy.wait_recv())
                start_z(i + AHEAD, jnp.minimum(i + AHEAD + 1, N))

            @pl.when(i == SUM_STEP)
            def _():
                sum_panel()

            @pl.when(i == COLUMNS_STEP)
            def _():
                pass_on_columns()

            c = fin[j] >> 1
            for dest in range(CHIPS):
                @pl.when(2 * dest + 1 >= col)
                def _():
                    if dest == 0:
                        src = zr.at[j, 0]
                    elif dest == 3:
                        src = zr.at[j, 2]
                    else:
                        src = xs.at[j, dest - 1]
                        later = (cb[c, 3 * row + dest] >> 4) == dest
                        src[...] = jnp.where(later, zr[j, dest], zr[j, dest - 1])

                    @pl.when(chip == dest)
                    def _():
                        xr[core, j, chip] = src[...]

                    @pl.when(chip != dest)
                    def _():
                        x_copy(j, src, dest, chip).start()

        @pl.when((i >= LAG) & needed)
        def _():
            before = (col + ring_offset(i - LAG)) % N
            for slot in range(CHIPS):
                @pl.when(chip != slot)
                def _():
                    x_copy(before, xs.at[before, 0], slot, slot).wait_recv()

            f_copy(before, core).start()

        @pl.when(i == FIRST_BLOCK)
        def _():
            @pl.when(row != 0)
            def _():
                co_copy(row).wait_recv()

            from_lower(a, co)

        @pl.when((i >= FIRST_BLOCK) & (i < FIRST_BLOCK + 4) & (row >= col))
        def _():
            @pl.loop(0, 2)
            def _(_i):
                sweep_block(a)

    @pl.when(row >= col)
    def _():
        @pl.loop(1, N)
        def _(i):
            b = (col + i) % N

            @pl.when((row > 0) | (b > 1))
            def _():
                pr_copy(b, b).wait_recv()

    out_t = pltpu.make_async_copy(t, t_o, o_s.at[0])
    out_pc = pltpu.make_async_copy(pc, pc_o, o_s.at[1])
    out_xr = pltpu.make_async_copy(xr, xr_o, o_s.at[2])

    @pl.when(row >= col)
    def _():
        times_inverse(t, pr, a)
        out_t.start()

        @pl.loop(1, N)
        def _(i):
            slot = (row + i) % N
            pc_copy(slot, slot).wait_recv()

        out_pc.start()

    @pl.when(needed)
    def _():
        @pl.loop(0, N)
        def _(j):
            f_copy(j, 1 - core).wait_recv()

    @pl.when(row >= col)
    def _():
        out_xr.start()
        out_xr.wait()
        out_t.wait()
        out_pc.wait()

    @pl.loop(1, N)
    def _(i):
        r = (row + i) % N
        c = (col + i) % N
        px_copy(r, row).wait_send()
        pz_copy(c, col).wait_send()
        z_copies(c, col, c, lambda copy: copy.wait_send())

        @pl.when((c <= row) | ((row == 0) & (col < 2)))
        def _():
            pr_copy(c, col).wait_send()

        @pl.when(r >= col)
        def _():
            pc_copy(r, row).wait_send()

        @pl.when(row == 0)
        def _():
            co_copy(r).wait_send()

    @pl.when(row != col)
    def _():
        pt_copy.wait_send()

    @pl.loop(0, N)
    def _(j):
        for dest in range(CHIPS):
            @pl.when((2 * dest + 1 >= col) & (chip != dest))
            def _():
                x_copy(j, xs.at[j, 0], dest, chip).wait_send()

        @pl.when(needed)
        def _():
            f_copy(j, core).wait_send()


def exchange(cb, live, fin, contrib, fcp):
    dma = pltpu.SemaphoreType.DMA
    any_ = pl.BlockSpec(memory_space=pl.ANY)
    vmem = pl.BlockSpec(memory_space=pltpu.VMEM)
    smem = pl.BlockSpec(memory_space=pltpu.SMEM)
    block = (BLK, BLK)
    panel = (BLK, PANEL)
    return pl.pallas_call(
        exchange_kernel,
        out_shape=[
            jax.ShapeDtypeStruct((2, N, CHIPS, 2, *block), BF16),
            jax.ShapeDtypeStruct((N, *panel), BF16),
            jax.ShapeDtypeStruct((N, *panel), BF16),
        ],
        in_specs=[smem, smem, smem, vmem, vmem],
        out_specs=[any_] * 3,
        scratch_shapes=[
            pltpu.VMEM((PANEL, PANEL), F32),
            pltpu.VMEM((N, *panel), BF16),
            pltpu.VMEM((N, *block), BF16),
            pltpu.VMEM((N, *block), BF16),
            pltpu.VMEM((N, BLK + 32, BLK), BF16),
            pltpu.VMEM((N, BLK + 32, BLK), BF16),
            pltpu.VMEM(panel, BF16),
            pltpu.VMEM((N, *panel), BF16),
            pltpu.VMEM(panel, BF16),
            pltpu.VMEM((N, *panel), BF16),
            pltpu.VMEM((2, *panel), BF16),
            pltpu.VMEM((N, 3, 2, *block), BF16),
            pltpu.VMEM((N, 3, 2, *block), BF16),
            pltpu.VMEM((N, 2, 2, *block), BF16),
            pltpu.VMEM((2, N, CHIPS, 2, *block), BF16),
            dma((N,)), dma((N,)),
            dma((N,)), dma((N,)),
            dma((N,)), dma((N,)),
            dma, dma,
            dma((N,)), dma((N,)),
            dma((N,)), dma,
            dma((N,)), dma((N,)),
            dma((N, CHIPS)), dma((N, CHIPS)),
            dma((N,)), dma((N,)),
            dma((3,)),
        ],
        compiler_params=pltpu.CompilerParams(
            collective_id=0, has_side_effects=True, vmem_limit_bytes=40 << 20
        ),
        name="exchange",
    )(cb, live, fin, contrib, fcp)


def update_kernel(cb, live, fin, xr, t, pc, out, total, rowq, colq, colc, jof):
    row = lax.axis_index("row")
    col = lax.axis_index("col")
    p = pl.program_id(0)

    @pl.when((p == 0) & (row >= col))
    def _():
        for i in range(4 * N):
            rowq[i] = -1
            colq[i] = -1
        for j in range(N):
            jof[fin[j]] = j
        for c in range(4):
            for q in range(BLOCKS):
                v = cb[c, q]
                m = 4 * (q % 3) + (q // 3) % 4
                before = q - q % 12 + 3 * ((m - 1) % 4) + (m - 1) // 4

                @pl.when(v >> 3 == row)
                def _():
                    rowq[N * c + (v & 7)] = q

                @pl.when(v >> 3 == col)
                def _():
                    colq[N * c + (v & 7)] = q
                    if m == 0:
                        colc[N * c + (v & 7)] = 0
                    else:
                        colc[N * c + (v & 7)] = jnp.where(cb[c, before] >> 3 == col, 1, 0)

    @pl.when(row < col)
    def _():
        out[...] = jnp.zeros_like(out)

    @pl.when(row >= col)
    def _():
        rows = t[p]
        for b in range(0, N, 2):
            columns = pc[b : b + 2].reshape(2 * BLK, PANEL)
            total[:, b * BLK : (b + 2) * BLK] = -lax.dot_general(
                rows, columns, (((1,), (1,)), ((), ())), preferred_element_type=F32
            )
        for c in range(4):
            q = rowq[N * c + p]

            @pl.when((q >= 0) & (q < live[c]))
            def _():
                r = q // 3
                for b in range(N):
                    s = colq[N * c + b]

                    @pl.when((s >= 0) & (s <= q))
                    def _():
                        j = jof[2 * c + jnp.where(s >= 12, 1, 0)]
                        block = xr[r % 2, j, r // 2, colc[N * c + b]]
                        total[:, b * BLK : (b + 1) * BLK] += block.astype(F32)

        ri = (N * row + p) * BLK + lax.broadcasted_iota(jnp.int32, (BLK, N * BLK), 0)
        ci = N * BLK * col + lax.broadcasted_iota(jnp.int32, (BLK, N * BLK), 1)
        keep = (ri >= ci) & (ri >= PANEL) & (ci >= PANEL)
        out[...] = jnp.where(keep, total[...], 0.0).astype(BF16)


def update(cb, live, fin, xr, t, pc):
    smem = pl.BlockSpec(memory_space=pltpu.SMEM)
    vmem = pl.BlockSpec(memory_space=pltpu.VMEM)
    ints = lambda n: pltpu.SMEM((n,), jnp.int32)
    return pl.pallas_call(
        update_kernel,
        grid=(N,),
        out_shape=jax.ShapeDtypeStruct((N * BLK, N * BLK), BF16),
        in_specs=[smem] * 3 + [vmem] * 3,
        out_specs=pl.BlockSpec((BLK, N * BLK), lambda p: (p, 0)),
        scratch_shapes=[
            pltpu.VMEM((BLK, N * BLK), F32),
            ints(4 * N), ints(4 * N), ints(4 * N), ints(N),
        ],
        compiler_params=pltpu.CompilerParams(vmem_limit_bytes=40 << 20),
        name="update",
    )(cb, live, fin, xr, t, pc)


def body(front_cols, contrib, child_blocks, child_live, finish):
    packed = front_cols.reshape(N, 4, 32, 32).transpose(0, 2, 1, 3).reshape(N, 32, BLK)
    pieces = contrib.reshape(3, BLK, 12 * BLK)
    xr, t, pc = exchange(child_blocks, child_live, finish, pieces, packed)
    return update(child_blocks, child_live, finish, xr, t, pc)


def solution(mesh):
    return jax.shard_map(
        body,
        mesh=mesh,
        in_specs=(
            P(("front", "row"), "col"),
            P(("front", "col"), "row", None),
            P("front", None),
            P("front"),
            P("front"),
        ),
        out_specs=P(("front", "row"), "col"),
        check_vma=False,
    )
```

```python
import jax
import jax.numpy as jnp
from jax import lax
from jax.experimental import pallas as pl
from jax.experimental.pallas import tpu as pltpu
from jax.sharding import PartitionSpec as P

BLK = 128
PANEL = 256
N = 8
CHIPS = 4
BLOCKS = 24
BF16 = jnp.bfloat16
F32 = jnp.float32
LAG = 2
EARLY = 3
BEFORE_SUM = 5
SUM_STEP = 3
COLUMNS_STEP = 5
FIRST_BLOCK = 4
RING_STEP = 5


def copy_to(src, dst, send, recv, **device):
    return pltpu.make_async_remote_copy(
        src_ref=src,
        dst_ref=dst,
        send_sem=send,
        recv_sem=recv,
        device_id=device,
        device_id_type=pl.DeviceIdType.MESH,
    )


def ring_offset(i):
    return jnp.where(i % 2 == 1, (i + 1) // 2, (N - i // 2) % N)


def first_kept(row, col):
    return jnp.maximum(col - 1 - (row % 4) // 2, 0) // 2


def chosen(cases):
    value = cases[0][1]
    for holds, other in cases[1:]:
        value = jnp.where(holds, other, value)
    return value


def column_block(m):
    place = 3 * (m % 4) + m // 4
    return slice(place * BLK, (place + 1) * BLK)


def dot(a, b):
    ah = a.astype(BF16)
    bh = b.astype(BF16)
    al = (a - ah.astype(F32)).astype(BF16)
    bl = (b - bh.astype(F32)).astype(BF16)
    return product(ah, bh) + (product(ah, bl) + product(al, bh))


def product(a, b):
    return jnp.dot(a, b, preferred_element_type=F32)


STEP = 32
TOGETHER = 8


def small_inverse(d):
    n = d.shape[0]
    rows = lax.broadcasted_iota(jnp.int32, (n, n), 0)
    cols = lax.broadcasted_iota(jnp.int32, (n, n), 1)
    for k in range(0, n, TOGETHER):
        down = [jnp.broadcast_to(d[:, k + i : k + i + 1], (n, n)) for i in range(TOGETHER)]
        across = [d[k + i : k + i + 1, :] for i in range(TOGETHER)]
        for p in range(TOGETHER):
            at = k + p
            base = down[p]
            inv = 1.0 / base[at : at + 1, :]
            scales = [base[k + i : k + i + 1, :] * inv for i in range(TOGETHER)]
            scaled = across[p] * inv
            d = d - base * scaled
            for i in range(TOGETHER):
                if i != p:
                    down[i] = jnp.where(rows == at, scales[i], down[i] - base * scales[i])
                    across[i] = across[i] - scales[i] * across[p]
            down[p] = jnp.where(rows == at, -inv, base * inv)
            across[p] = scaled
        for i in range(TOGETHER):
            d = jnp.where(rows == k + i, across[i], d)
        for i in range(TOGETHER):
            d = jnp.where(cols == k + i, down[i], d)
    return -d


def sweep_block(a):
    across = a[0:STEP, :]
    down = a[:, 0:STEP]
    inv = small_inverse(a[0:STEP, 0:STEP])
    q = dot(inv, across)
    qt = dot(down, inv)
    a[...] = a[...] - dot(qt, across)
    a[0:STEP, :] = q
    a[:, 0:STEP] = qt
    a[0:STEP, 0:STEP] = -inv
    n = a.shape[0]
    a[...] = pltpu.roll(pltpu.roll(a[...], n - STEP, 0), n - STEP, 1)


def from_lower(a, co):
    lower = jnp.concatenate([co[0], co[1]], axis=0).astype(F32)
    ri = lax.broadcasted_iota(jnp.int32, (PANEL, PANEL), 0)
    ci = lax.broadcasted_iota(jnp.int32, (PANEL, PANEL), 1)
    a[...] = lower + jnp.where(ri < ci, lower.T, 0.0)


def times_inverse(t, pr, a):
    m = -a[...]
    high = m.astype(BF16)
    low = (m - high.astype(F32)).astype(BF16)
    for b in range(0, N, 2):
        rows = pr[b : b + 2].reshape(2 * BLK, PANEL)
        both = product(rows, high) + product(rows, low)
        t[b : b + 2] = both.astype(BF16).reshape(2, BLK, PANEL)


def exchange_kernel(
    cb, live, fin, contrib, fcp,
    xr, t, pc,
    a, px, pxr, pz, pzr, pb, pr, pt, co, zs, zr, xs,
    px_s, px_r, pz_s, pz_r, pr_s, pr_r, t_s, t_r, pc_s, pc_r, co_s, co_r,
    z_s, z_r, x_s, x_r, f_s, f_r,
):
    row = lax.axis_index("row")
    col = lax.axis_index("col")
    chip = row // 2
    core = row % 2
    mate = 2 * chip + 1 - core

    barrier = pltpu.get_barrier_semaphore()

    @pl.loop(1, N)
    def _(d):
        pl.semaphore_signal(barrier, 1, device_id={"row": (row + d) % N}, device_id_type=pl.DeviceIdType.MESH)
        pl.semaphore_signal(barrier, 1, device_id={"col": (col + d) % N}, device_id_type=pl.DeviceIdType.MESH)

    @pl.when(row != col)
    def _():
        pl.semaphore_signal(barrier, 1, device_id={"row": col, "col": row}, device_id_type=pl.DeviceIdType.MESH)

    piece = fin[col]
    child = piece >> 1
    half = piece & 1
    groups = [cb[child, 3 * row + k] >> 3 for k in range(3)]
    for dest in range(N):
        px[dest] = chosen([(groups[k] == dest, contrib[k, :, 0:BLK]) for k in range(3)])
    pxr[row] = px[row]

    @pl.when(row == col)
    def _():
        pl.semaphore_wait(barrier, 2 * N - 2)

    @pl.when(row != col)
    def _():
        pl.semaphore_wait(barrier, 2 * N - 1)

    def px_copy(dest, slot):
        return copy_to(px.at[dest], pxr.at[slot], px_s.at[dest], px_r.at[slot], row=dest)

    @pl.loop(1, N)
    def _(d):
        dest = (row + d) % N
        px_copy(dest, row).start()

    col_groups = [cb[child, 12 * half + 3 * (m % 4) + m // 4] >> 3 for m in range(12)]
    for dest in range(N):
        first = sum(jnp.where(g < dest, 1, 0) for g in col_groups)
        for k in range(0 if dest < 4 else 1 if dest < 6 else 2, 3):
            for c in range(2):
                ms = range(max(0, 2 * dest - 4 + c), min(2 * dest + 1, 4 * k + 3) + 1)
                zs[dest, k, c] = chosen([(first == m - c, contrib[k, :, column_block(m)]) for m in ms])
    zr[col] = zs[col]

    def z_copies(dest, slot, by, act):
        for k in range(3):
            @pl.when(first_kept(row, by) == k)
            def _():
                act(copy_to(
                    zs.at[dest, pl.ds(k, 3 - k)], zr.at[slot, pl.ds(k, 3 - k)],
                    z_s.at[dest], z_r.at[slot], col=dest,
                ))

    def start_z(first, end):
        @pl.loop(first, end)
        def _(i):
            dest = (col + ring_offset(i)) % N
            z_copies(dest, col, dest, lambda copy: copy.start())

    start_z(1, EARLY)

    from_row = [jnp.int32(0)] * N
    for q in range(BLOCKS):
        at = cb[child, q] - N * row
        from_row = [jnp.where(at == b, q // 3, from_row[b]) for b in range(N)]

    @pl.loop(1, N)
    def _(d):
        px_copy((row + d) % N, (row + d) % N).wait_recv()

    for b in range(N):
        pz[b, 0:BLK] = chosen([(from_row[b] == r, pxr[r]) for r in range(N)])
        pz[b, BLK:] = fcp[b]
    pzr[col] = pz[col]

    def pz_copy(dest, slot):
        return copy_to(pz.at[dest], pzr.at[slot], pz_s.at[dest], pz_r.at[slot], col=dest)

    @pl.loop(0, N)
    def _(i):
        dest = jnp.where(row == 0, i, (col + ring_offset(i)) % N)

        @pl.when(dest != col)
        def _():
            pz_copy(dest, col).start()

    start_z(EARLY, BEFORE_SUM)

    def pr_copy(dest, slot):
        return copy_to(pb, pr.at[slot], pr_s.at[dest], pr_r.at[slot], col=dest)

    pt_copy = copy_to(pb, pt, t_s, t_r, row=col, col=row)

    def co_copy(dest):
        return copy_to(pr.at[pl.ds(0, 2)], co, co_s.at[dest], co_r, row=dest)

    def ring_copy(s, right):
        if right:
            block, dest = (col + N - s) % N, (col + 1) % N
        else:
            block, dest = (col + s) % N, (col + N - 1) % N
        sem = pr_s.at[s if right else 4 + s]
        return copy_to(pr.at[block], pr.at[block], sem, pr_r.at[block], col=dest)

    def ring_step(s):
        for right in (True, False):
            if s > 0:
                ring_copy(s, right).wait_recv()
            if right or s < 3:
                ring_copy(s, right).start()

    def sum_panel():
        @pl.loop(1, N)
        def _(i):
            pz_copy((col + i) % N, (col + i) % N).wait_recv()

        left = jnp.zeros((BLK, BLK), F32)
        right = jnp.zeros((BLK, BLK), F32)
        for j in range(N):
            c = fin[j] >> 1
            column = 12 * (fin[j] & 1)
            q = jnp.int32(-1)
            for entry in range(BLOCKS):
                q = jnp.where(cb[c, entry] == N * row + col, entry, q)
            at = cb[c, column]
            valid = (q >= column) & (q < live[c])
            block = pzr[j, 0:BLK].astype(F32)
            left += jnp.where(valid & (at == 0), block, 0.0)
            right += jnp.where(valid & (at == 1), block, 0.0)
        lane = lax.broadcasted_iota(jnp.int32, (32, BLK), 1) // 32
        packed = [pzr[j, BLK:].astype(F32) for j in range(N)]
        for s in range(4):
            parts = []
            for side in range(2):
                part = jnp.zeros((32, BLK), F32)
                for j in range(4):
                    moved = packed[4 * side + j]
                    if (j - s) % 4:
                        moved = pltpu.roll(moved, 32 * ((j - s) % 4), 1)
                    part = jnp.where(lane == j, moved, part)
                parts.append(part)
            rows = slice(32 * s, 32 * s + 32)
            row_ids = (N * row + col) * BLK + 32 * s + lax.broadcasted_iota(jnp.int32, (32, BLK), 0)
            col_ids = lax.broadcasted_iota(jnp.int32, (32, BLK), 1)
            pb[rows, 0:BLK] = jnp.where(row_ids >= col_ids, left[rows] + parts[0], 0.0).astype(BF16)
            pb[rows, BLK:] = jnp.where(row_ids >= col_ids + BLK, right[rows] + parts[1], 0.0).astype(BF16)
        pr[col] = pb[...]

        @pl.when(row == 0)
        def _():
            @pl.loop(1, N)
            def _(i):
                dest = (col + ring_offset(i)) % N

                @pl.when((dest == 0) | (col < 2))
                def _():
                    pr_copy(dest, col).start()

        @pl.when(row > 0)
        def _():
            ring_step(0)

        @pl.when(row != col)
        def _():
            pt_copy.start()

        @pl.when(row == col)
        def _():
            pt[...] = pb[...]

        start_z(BEFORE_SUM, N)

        @pl.when(row == 0)
        def _():
            for b in range(2):
                @pl.when(col != b)
                def _():
                    pr_copy(b, b).wait_recv()

            @pl.loop(1, N)
            def _(dest):
                co_copy(dest).start()

            co[...] = pr[0:2]

    def pc_copy(dest, slot):
        return copy_to(pt, pc.at[slot], pc_s.at[dest], pc_r.at[slot], row=dest)

    def pass_on_columns():
        @pl.when(row != col)
        def _():
            pt_copy.wait_recv()

        @pl.loop(1, N)
        def _(i):
            dest = (row + i) % N

            @pl.when(dest >= col)
            def _():
                pc_copy(dest, row).start()

        pc[row] = pt[...]

    needed = chip >= col // 2

    def x_copy(j, src, dest, slot):
        return copy_to(src, xr.at[core, j, slot], x_s.at[j, dest], x_r.at[j, slot], row=2 * dest + core)

    def f_copy(j, side):
        return copy_to(xr.at[side, j], xr.at[side, j], f_s.at[j], f_r.at[j], row=mate)

    @pl.loop(0, N + LAG)
    def _(i):
        j = (col + ring_offset(i)) % N

        @pl.when(i < N)
        def _():
            @pl.when(i == SUM_STEP)
            def _():
                sum_panel()

            @pl.when(i == COLUMNS_STEP)
            def _():
                pass_on_columns()

            for s in range(1, 4):
                @pl.when((i == RING_STEP + s - 1) & (row > 0))
                def _():
                    ring_step(s)

            @pl.when(i > 0)
            def _():
                z_copies(j, j, col, lambda copy: copy.wait_recv())

            c = fin[j] >> 1
            for dest in range(CHIPS):
                @pl.when(2 * dest + 1 >= col)
                def _():
                    if dest == 0:
                        src = zr.at[j, 0]
                    elif dest == 3:
                        src = zr.at[j, 2]
                    else:
                        src = xs.at[j, dest - 1]
                        later = (cb[c, 3 * row + dest] >> 4) == dest
                        src[...] = jnp.where(later, zr[j, dest], zr[j, dest - 1])

                    @pl.when(chip == dest)
                    def _():
                        xr[core, j, chip] = src[...]

                    @pl.when(chip != dest)
                    def _():
                        x_copy(j, src, dest, chip).start()

        @pl.when((i >= LAG) & needed)
        def _():
            before = (col + ring_offset(i - LAG)) % N
            for slot in range(CHIPS):
                @pl.when(chip != slot)
                def _():
                    x_copy(before, xs.at[before, 0], slot, slot).wait_recv()

            f_copy(before, core).start()

        @pl.when(i == FIRST_BLOCK)
        def _():
            @pl.when(row != 0)
            def _():
                co_copy(row).wait_recv()

            from_lower(a, co)

        @pl.when((i >= FIRST_BLOCK) & (i < FIRST_BLOCK + 4) & (row >= col))
        def _():
            @pl.loop(0, 2)
            def _(_i):
                sweep_block(a)

    @pl.when(row > 0)
    def _():
        last = (col + 4) % N
        pr_copy(last, last).wait_recv()

    @pl.when((row == 0) & (col == 0))
    def _():
        @pl.loop(2, N)
        def _(b):
            pr_copy(b, b).wait_recv()

    @pl.when(row >= col)
    def _():
        times_inverse(t, pr, a)

        @pl.loop(1, N)
        def _(i):
            slot = (row + i) % N
            pc_copy(slot, slot).wait_recv()

    @pl.when(needed)
    def _():
        @pl.loop(0, N)
        def _(j):
            f_copy(j, 1 - core).wait_recv()

    @pl.loop(1, N)
    def _(i):
        r = (row + i) % N
        c = (col + i) % N
        px_copy(r, row).wait_send()
        pz_copy(c, col).wait_send()
        z_copies(c, col, c, lambda copy: copy.wait_send())

        @pl.when((row == 0) & ((c == 0) | (col < 2)))
        def _():
            pr_copy(c, col).wait_send()

        @pl.when(r >= col)
        def _():
            pc_copy(r, row).wait_send()

        @pl.when(row == 0)
        def _():
            co_copy(r).wait_send()

    @pl.when(row > 0)
    def _():
        for s in range(4):
            ring_copy(s, True).wait_send()
            if s < 3:
                ring_copy(s, False).wait_send()

    @pl.when(row != col)
    def _():
        pt_copy.wait_send()

    @pl.loop(0, N)
    def _(j):
        for dest in range(CHIPS):
            @pl.when((2 * dest + 1 >= col) & (chip != dest))
            def _():
                x_copy(j, xs.at[j, 0], dest, chip).wait_send()

        @pl.when(needed)
        def _():
            f_copy(j, core).wait_send()


def exchange(cb, live, fin, contrib, fcp):
    dma = pltpu.SemaphoreType.DMA
    vmem = pl.BlockSpec(memory_space=pltpu.VMEM)
    smem = pl.BlockSpec(memory_space=pltpu.SMEM)
    block = (BLK, BLK)
    panel = (BLK, PANEL)
    return pl.pallas_call(
        exchange_kernel,
        out_shape=[
            jax.ShapeDtypeStruct((2, N, CHIPS, 2, *block), BF16),
            jax.ShapeDtypeStruct((N, *panel), BF16),
            jax.ShapeDtypeStruct((N, *panel), BF16),
        ],
        in_specs=[smem, smem, smem, vmem, vmem],
        out_specs=[vmem] * 3,
        scratch_shapes=[
            pltpu.VMEM((PANEL, PANEL), F32),
            pltpu.VMEM((N, *block), BF16),
            pltpu.VMEM((N, *block), BF16),
            pltpu.VMEM((N, BLK + 32, BLK), BF16),
            pltpu.VMEM((N, BLK + 32, BLK), BF16),
            pltpu.VMEM(panel, BF16),
            pltpu.VMEM((N, *panel), BF16),
            pltpu.VMEM(panel, BF16),
            pltpu.VMEM((2, *panel), BF16),
            pltpu.VMEM((N, 3, 2, *block), BF16),
            pltpu.VMEM((N, 3, 2, *block), BF16),
            pltpu.VMEM((N, 2, 2, *block), BF16),
            dma((N,)), dma((N,)),
            dma((N,)), dma((N,)),
            dma((N,)), dma((N,)),
            dma, dma,
            dma((N,)), dma((N,)),
            dma((N,)), dma,
            dma((N,)), dma((N,)),
            dma((N, CHIPS)), dma((N, CHIPS)),
            dma((N,)), dma((N,)),
        ],
        compiler_params=pltpu.CompilerParams(
            collective_id=0, has_side_effects=True, vmem_limit_bytes=40 << 20
        ),
        name="exchange",
    )(cb, live, fin, contrib, fcp)


def update_kernel(cb, live, fin, xr, t, pc, out, total, strip, rowq, colq, colc, jof, sem):
    row = lax.axis_index("row")
    col = lax.axis_index("col")

    def strip_copy(p):
        rows = pl.ds(pl.multiple_of(p * BLK, BLK), BLK)
        return pltpu.make_async_copy(strip.at[p % 2], out.at[rows], sem.at[p % 2])

    @pl.when(row >= col)
    def _():
        for i in range(4 * N):
            rowq[i] = -1
            colq[i] = -1
        for j in range(N):
            jof[fin[j]] = j
        for c in range(4):
            for q in range(BLOCKS):
                v = cb[c, q]
                m = 4 * (q % 3) + (q // 3) % 4
                before = q - q % 12 + 3 * ((m - 1) % 4) + (m - 1) // 4

                @pl.when(v >> 3 == row)
                def _():
                    rowq[N * c + (v & 7)] = q

                @pl.when(v >> 3 == col)
                def _():
                    colq[N * c + (v & 7)] = q
                    if m == 0:
                        colc[N * c + (v & 7)] = 0
                    else:
                        colc[N * c + (v & 7)] = jnp.where(cb[c, before] >> 3 == col, 1, 0)

    def one_strip(p):
        rows = t[p]
        for b in range(0, N, 2):
            columns = pc[b : b + 2].reshape(2 * BLK, PANEL)
            total[:, b * BLK : (b + 2) * BLK] = -lax.dot_general(
                rows, columns, (((1,), (1,)), ((), ())), preferred_element_type=F32
            )
        for c in range(4):
            q = rowq[N * c + p]

            @pl.when((q >= 0) & (q < live[c]))
            def _():
                r = q // 3
                for b in range(N):
                    s = colq[N * c + b]

                    @pl.when((s >= 0) & (s <= q))
                    def _():
                        j = jof[2 * c + jnp.where(s >= 12, 1, 0)]
                        block = xr[r % 2, j, r // 2, colc[N * c + b]]
                        total[:, b * BLK : (b + 1) * BLK] += block.astype(F32)

        ri = (N * row + p) * BLK + lax.broadcasted_iota(jnp.int32, (BLK, N * BLK), 0)
        ci = N * BLK * col + lax.broadcasted_iota(jnp.int32, (BLK, N * BLK), 1)
        keep = (ri >= ci) & (ri >= PANEL) & (ci >= PANEL)
        strip[p % 2] = jnp.where(keep, total[...], 0.0).astype(BF16)

    @pl.when(row < col)
    def _():
        strip[...] = jnp.zeros_like(strip)

    @pl.loop(0, N)
    def _(p):
        @pl.when(p >= 2)
        def _():
            strip_copy(p - 2).wait()

        @pl.when(row >= col)
        def _():
            one_strip(p)

        strip_copy(p).start()

    for p in range(N - 2, N):
        strip_copy(p).wait()


def update(cb, live, fin, xr, t, pc):
    smem = pl.BlockSpec(memory_space=pltpu.SMEM)
    vmem = pl.BlockSpec(memory_space=pltpu.VMEM)
    ints = lambda n: pltpu.SMEM((n,), jnp.int32)
    return pl.pallas_call(
        update_kernel,
        out_shape=jax.ShapeDtypeStruct((N * BLK, N * BLK), BF16),
        in_specs=[smem] * 3 + [vmem] * 3,
        out_specs=pl.BlockSpec(memory_space=pl.ANY),
        scratch_shapes=[
            pltpu.VMEM((BLK, N * BLK), F32),
            pltpu.VMEM((2, BLK, N * BLK), BF16),
            ints(4 * N), ints(4 * N), ints(4 * N), ints(N),
            pltpu.SemaphoreType.DMA((2,)),
        ],
        compiler_params=pltpu.CompilerParams(vmem_limit_bytes=40 << 20),
        name="update",
    )(cb, live, fin, xr, t, pc)


def body(front_cols, contrib, child_blocks, child_live, finish):
    packed = front_cols.reshape(N, 4, 32, 32).transpose(0, 2, 1, 3).reshape(N, 32, BLK)
    pieces = contrib.reshape(3, BLK, 12 * BLK)
    xr, t, pc = exchange(child_blocks, child_live, finish, pieces, packed)
    return update(child_blocks, child_live, finish, xr, t, pc)


def solution(mesh):
    return jax.shard_map(
        body,
        mesh=mesh,
        in_specs=(
            P(("front", "row"), "col"),
            P(("front", "col"), "row", None),
            P("front", None),
            P("front"),
            P("front"),
        ),
        out_specs=P(("front", "row"), "col"),
        check_vma=False,
    )
```

```python
import jax
import jax.numpy as jnp
from jax import lax
from jax.experimental import pallas as pl
from jax.experimental.pallas import tpu as pltpu
from jax.sharding import PartitionSpec as P

BLK = 128
PANEL = 256
N = 8
CHIPS = 4
BLOCKS = 24
BF16 = jnp.bfloat16
F32 = jnp.float32
LAG = 2
EARLY = 3
BEFORE_SUM = 5
SUM_STEP = 3
COLUMNS_STEP = 5
FIRST_BLOCK = 4
RING_STEP = 5


def copy_to(src, dst, send, recv, **device):
    return pltpu.make_async_remote_copy(
        src_ref=src,
        dst_ref=dst,
        send_sem=send,
        recv_sem=recv,
        device_id=device,
        device_id_type=pl.DeviceIdType.MESH,
    )


def ring_offset(i):
    return jnp.where(i % 2 == 1, (i + 1) // 2, (N - i // 2) % N)


def first_kept(row, col):
    return jnp.maximum(col - 1 - (row % 4) // 2, 0) // 2


def chosen(cases):
    value = cases[0][1]
    for holds, other in cases[1:]:
        value = jnp.where(holds, other, value)
    return value


def column_block(m):
    place = 3 * (m % 4) + m // 4
    return slice(place * BLK, (place + 1) * BLK)


def dot(a, b):
    ah = a.astype(BF16)
    bh = b.astype(BF16)
    al = (a - ah.astype(F32)).astype(BF16)
    bl = (b - bh.astype(F32)).astype(BF16)
    return product(ah, bh) + (product(ah, bl) + product(al, bh))


def product(a, b):
    return jnp.dot(a, b, preferred_element_type=F32)


STEP = 32
TOGETHER = 8


def small_inverse(d):
    n = d.shape[0]
    rows = lax.broadcasted_iota(jnp.int32, (n, n), 0)
    cols = lax.broadcasted_iota(jnp.int32, (n, n), 1)
    for k in range(0, n, TOGETHER):
        down = [jnp.broadcast_to(d[:, k + i : k + i + 1], (n, n)) for i in range(TOGETHER)]
        across = [d[k + i : k + i + 1, :] for i in range(TOGETHER)]
        for p in range(TOGETHER):
            at = k + p
            base = down[p]
            inv = 1.0 / base[at : at + 1, :]
            scales = [base[k + i : k + i + 1, :] * inv for i in range(TOGETHER)]
            scaled = across[p] * inv
            d = d - base * scaled
            for i in range(TOGETHER):
                if i != p:
                    down[i] = jnp.where(rows == at, scales[i], down[i] - base * scales[i])
                    across[i] = across[i] - scales[i] * across[p]
            down[p] = jnp.where(rows == at, -inv, base * inv)
            across[p] = scaled
        for i in range(TOGETHER):
            d = jnp.where(rows == k + i, across[i], d)
        for i in range(TOGETHER):
            d = jnp.where(cols == k + i, down[i], d)
    return -d


def sweep_block(a):
    across = a[0:STEP, :]
    down = a[:, 0:STEP]
    inv = small_inverse(a[0:STEP, 0:STEP])
    q = dot(inv, across)
    qt = dot(down, inv)
    a[...] = a[...] - dot(qt, across)
    a[0:STEP, :] = q
    a[:, 0:STEP] = qt
    a[0:STEP, 0:STEP] = -inv
    n = a.shape[0]
    a[...] = pltpu.roll(pltpu.roll(a[...], n - STEP, 0), n - STEP, 1)


def from_lower(a, co):
    lower = jnp.concatenate([co[0], co[1]], axis=0).astype(F32)
    ri = lax.broadcasted_iota(jnp.int32, (PANEL, PANEL), 0)
    ci = lax.broadcasted_iota(jnp.int32, (PANEL, PANEL), 1)
    a[...] = lower + jnp.where(ri < ci, lower.T, 0.0)


def times_inverse(t, pr, a):
    m = -a[...]
    high = m.astype(BF16)
    low = (m - high.astype(F32)).astype(BF16)
    for b in range(0, N, 2):
        rows = pr[b : b + 2].reshape(2 * BLK, PANEL)
        both = product(rows, high) + product(rows, low)
        t[b : b + 2] = both.astype(BF16).reshape(2, BLK, PANEL)


def exchange_kernel(
    cb, live, fin, contrib, fct,
    xr, t, pc,
    a, px, pxr, pz, pzr, pb, pr, pt, co, zs, zr, xs,
    px_s, px_r, pz_s, pz_r, pr_s, pr_r, t_s, t_r, pc_s, pc_r, co_s, co_r,
    z_s, z_r, x_s, x_r, f_s, f_r,
):
    row = lax.axis_index("row")
    col = lax.axis_index("col")
    chip = row // 2
    core = row % 2
    mate = 2 * chip + 1 - core

    barrier = pltpu.get_barrier_semaphore()

    @pl.loop(1, N)
    def _(d):
        pl.semaphore_signal(barrier, 1, device_id={"row": (row + d) % N}, device_id_type=pl.DeviceIdType.MESH)
        pl.semaphore_signal(barrier, 1, device_id={"col": (col + d) % N}, device_id_type=pl.DeviceIdType.MESH)

    @pl.when(row != col)
    def _():
        pl.semaphore_signal(barrier, 1, device_id={"row": col, "col": row}, device_id_type=pl.DeviceIdType.MESH)

    piece = fin[col]
    child = piece >> 1
    half = piece & 1
    groups = [cb[child, 3 * row + k] >> 3 for k in range(3)]
    for dest in range(N):
        px[dest] = chosen([(groups[k] == dest, contrib[k, :, 0:BLK]) for k in range(3)])
    pxr[row] = px[row]

    @pl.when(row == col)
    def _():
        pl.semaphore_wait(barrier, 2 * N - 2)

    @pl.when(row != col)
    def _():
        pl.semaphore_wait(barrier, 2 * N - 1)

    def px_copy(dest, slot):
        return copy_to(px.at[dest], pxr.at[slot], px_s.at[dest], px_r.at[slot], row=dest)

    @pl.loop(1, N)
    def _(d):
        dest = (row + d) % N
        px_copy(dest, row).start()

    col_groups = [cb[child, 12 * half + 3 * (m % 4) + m // 4] >> 3 for m in range(12)]
    for dest in range(N):
        first = sum(jnp.where(g < dest, 1, 0) for g in col_groups)
        for k in range(0 if dest < 4 else 1 if dest < 6 else 2, 3):
            for c in range(2):
                ms = range(max(0, 2 * dest - 4 + c), min(2 * dest + 1, 4 * k + 3) + 1)
                zs[dest, k, c] = chosen([(first == m - c, contrib[k, :, column_block(m)]) for m in ms])
    zr[col] = zs[col]

    def z_copies(dest, slot, by, act):
        for k in range(3):
            @pl.when(first_kept(row, by) == k)
            def _():
                act(copy_to(
                    zs.at[dest, pl.ds(k, 3 - k)], zr.at[slot, pl.ds(k, 3 - k)],
                    z_s.at[dest], z_r.at[slot], col=dest,
                ))

    def start_z(first, end):
        @pl.loop(first, end)
        def _(i):
            dest = (col + ring_offset(i)) % N
            z_copies(dest, col, dest, lambda copy: copy.start())

    start_z(1, EARLY)

    from_row = [jnp.int32(0)] * N
    for q in range(BLOCKS):
        at = cb[child, q] - N * row
        from_row = [jnp.where(at == b, q // 3, from_row[b]) for b in range(N)]

    @pl.loop(1, N)
    def _(d):
        px_copy((row + d) % N, (row + d) % N).wait_recv()

    for b in range(N):
        pz[b, 0:BLK] = chosen([(from_row[b] == r, pxr[r]) for r in range(N)])
        pz[b, BLK:] = fct[:, b * BLK : (b + 1) * BLK]
    pzr[col] = pz[col]

    def pz_copy(dest, slot):
        return copy_to(pz.at[dest], pzr.at[slot], pz_s.at[dest], pz_r.at[slot], col=dest)

    @pl.loop(0, N)
    def _(i):
        dest = jnp.where(row == 0, i, (col + ring_offset(i)) % N)

        @pl.when(dest != col)
        def _():
            pz_copy(dest, col).start()

    start_z(EARLY, BEFORE_SUM)

    def pr_copy(dest, slot):
        return copy_to(pb, pr.at[slot], pr_s.at[dest], pr_r.at[slot], col=dest)

    pt_copy = copy_to(pb, pt, t_s, t_r, row=col, col=row)

    def co_copy(dest):
        return copy_to(pr.at[pl.ds(0, 2)], co, co_s.at[dest], co_r, row=dest)

    def ring_copy(s, right):
        if right:
            block, dest = (col + N - s) % N, (col + 1) % N
        else:
            block, dest = (col + s) % N, (col + N - 1) % N
        sem = pr_s.at[s if right else 4 + s]
        return copy_to(pr.at[block], pr.at[block], sem, pr_r.at[block], col=dest)

    def ring_step(s):
        for right in (True, False):
            if s > 0:
                ring_copy(s, right).wait_recv()
            if right or s < 3:
                ring_copy(s, right).start()

    def sum_panel():
        @pl.loop(1, N)
        def _(i):
            pz_copy((col + i) % N, (col + i) % N).wait_recv()

        left = jnp.zeros((BLK, BLK), F32)
        right = jnp.zeros((BLK, BLK), F32)
        for j in range(N):
            c = fin[j] >> 1
            column = 12 * (fin[j] & 1)
            q = jnp.int32(-1)
            for entry in range(BLOCKS):
                q = jnp.where(cb[c, entry] == N * row + col, entry, q)
            at = cb[c, column]
            valid = (q >= column) & (q < live[c])
            block = pzr[j, 0:BLK].astype(F32)
            left += jnp.where(valid & (at == 0), block, 0.0)
            right += jnp.where(valid & (at == 1), block, 0.0)
        initial = jnp.concatenate([pzr[j, BLK:] for j in range(N)], axis=0).astype(F32).T
        row_ids = (N * row + col) * BLK + lax.broadcasted_iota(jnp.int32, (BLK, PANEL), 0)
        col_ids = lax.broadcasted_iota(jnp.int32, (BLK, PANEL), 1)
        total = jnp.concatenate([left, right], axis=1) + initial
        pb[...] = jnp.where(row_ids >= col_ids, total, 0.0).astype(BF16)
        pr[col] = pb[...]

        @pl.when(row == 0)
        def _():
            @pl.loop(1, N)
            def _(i):
                dest = (col + ring_offset(i)) % N

                @pl.when((dest == 0) | (col < 2))
                def _():
                    pr_copy(dest, col).start()

        @pl.when(row > 0)
        def _():
            ring_step(0)

        @pl.when(row != col)
        def _():
            pt_copy.start()

        @pl.when(row == col)
        def _():
            pt[...] = pb[...]

        start_z(BEFORE_SUM, N)

        @pl.when(row == 0)
        def _():
            for b in range(2):
                @pl.when(col != b)
                def _():
                    pr_copy(b, b).wait_recv()

            @pl.loop(1, N)
            def _(dest):
                co_copy(dest).start()

            co[...] = pr[0:2]

    def pc_copy(dest, slot):
        return copy_to(pt, pc.at[slot], pc_s.at[dest], pc_r.at[slot], row=dest)

    def pass_on_columns():
        @pl.when(row != col)
        def _():
            pt_copy.wait_recv()

        @pl.loop(1, N)
        def _(i):
            dest = (row + i) % N

            @pl.when(dest >= col)
            def _():
                pc_copy(dest, row).start()

        pc[row] = pt[...]

    needed = chip >= col // 2

    def x_copy(j, src, dest, slot):
        return copy_to(src, xr.at[core, j, slot], x_s.at[j, dest], x_r.at[j, slot], row=2 * dest + core)

    def f_copy(j, side):
        return copy_to(xr.at[side, j], xr.at[side, j], f_s.at[j], f_r.at[j], row=mate)

    @pl.loop(0, N + LAG)
    def _(i):
        j = (col + ring_offset(i)) % N

        @pl.when(i < N)
        def _():
            @pl.when(i == SUM_STEP)
            def _():
                sum_panel()

            @pl.when(i == COLUMNS_STEP)
            def _():
                pass_on_columns()

            for s in range(1, 4):
                @pl.when((i == RING_STEP + s - 1) & (row > 0))
                def _():
                    ring_step(s)

            @pl.when(i > 0)
            def _():
                z_copies(j, j, col, lambda copy: copy.wait_recv())

            c = fin[j] >> 1
            for dest in range(CHIPS):
                @pl.when(2 * dest + 1 >= col)
                def _():
                    if dest == 0:
                        src = zr.at[j, 0]
                    elif dest == 3:
                        src = zr.at[j, 2]
                    else:
                        src = xs.at[j, dest - 1]
                        later = (cb[c, 3 * row + dest] >> 4) == dest
                        src[...] = jnp.where(later, zr[j, dest], zr[j, dest - 1])

                    @pl.when(chip == dest)
                    def _():
                        xr[core, j, chip] = src[...]

                    @pl.when(chip != dest)
                    def _():
                        x_copy(j, src, dest, chip).start()

        @pl.when((i >= LAG) & needed)
        def _():
            before = (col + ring_offset(i - LAG)) % N
            for slot in range(CHIPS):
                @pl.when(chip != slot)
                def _():
                    x_copy(before, xs.at[before, 0], slot, slot).wait_recv()

            f_copy(before, core).start()

        @pl.when(i == FIRST_BLOCK)
        def _():
            @pl.when(row != 0)
            def _():
                co_copy(row).wait_recv()

            from_lower(a, co)

        @pl.when((i >= FIRST_BLOCK) & (i < FIRST_BLOCK + 4) & (row >= col))
        def _():
            @pl.loop(0, 2)
            def _(_i):
                sweep_block(a)

    @pl.when(row > 0)
    def _():
        last = (col + 4) % N
        pr_copy(last, last).wait_recv()

    @pl.when((row == 0) & (col == 0))
    def _():
        @pl.loop(2, N)
        def _(b):
            pr_copy(b, b).wait_recv()

    @pl.when(row >= col)
    def _():
        times_inverse(t, pr, a)

        @pl.loop(1, N)
        def _(i):
            slot = (row + i) % N
            pc_copy(slot, slot).wait_recv()

    @pl.when(needed)
    def _():
        @pl.loop(0, N)
        def _(j):
            f_copy(j, 1 - core).wait_recv()

    @pl.loop(1, N)
    def _(i):
        r = (row + i) % N
        c = (col + i) % N
        px_copy(r, row).wait_send()
        pz_copy(c, col).wait_send()
        z_copies(c, col, c, lambda copy: copy.wait_send())

        @pl.when((row == 0) & ((c == 0) | (col < 2)))
        def _():
            pr_copy(c, col).wait_send()

        @pl.when(r >= col)
        def _():
            pc_copy(r, row).wait_send()

        @pl.when(row == 0)
        def _():
            co_copy(r).wait_send()

    @pl.when(row > 0)
    def _():
        for s in range(4):
            ring_copy(s, True).wait_send()
            if s < 3:
                ring_copy(s, False).wait_send()

    @pl.when(row != col)
    def _():
        pt_copy.wait_send()

    @pl.loop(0, N)
    def _(j):
        for dest in range(CHIPS):
            @pl.when((2 * dest + 1 >= col) & (chip != dest))
            def _():
                x_copy(j, xs.at[j, 0], dest, chip).wait_send()

        @pl.when(needed)
        def _():
            f_copy(j, core).wait_send()


def exchange(cb, live, fin, contrib, fct):
    dma = pltpu.SemaphoreType.DMA
    vmem = pl.BlockSpec(memory_space=pltpu.VMEM)
    smem = pl.BlockSpec(memory_space=pltpu.SMEM)
    block = (BLK, BLK)
    panel = (BLK, PANEL)
    return pl.pallas_call(
        exchange_kernel,
        out_shape=[
            jax.ShapeDtypeStruct((2, N, CHIPS, 2, *block), BF16),
            jax.ShapeDtypeStruct((N, *panel), BF16),
            jax.ShapeDtypeStruct((N, *panel), BF16),
        ],
        in_specs=[smem, smem, smem, vmem, vmem],
        out_specs=[vmem] * 3,
        scratch_shapes=[
            pltpu.VMEM((PANEL, PANEL), F32),
            pltpu.VMEM((N, *block), BF16),
            pltpu.VMEM((N, *block), BF16),
            pltpu.VMEM((N, BLK + 32, BLK), BF16),
            pltpu.VMEM((N, BLK + 32, BLK), BF16),
            pltpu.VMEM(panel, BF16),
            pltpu.VMEM((N, *panel), BF16),
            pltpu.VMEM(panel, BF16),
            pltpu.VMEM((2, *panel), BF16),
            pltpu.VMEM((N, 3, 2, *block), BF16),
            pltpu.VMEM((N, 3, 2, *block), BF16),
            pltpu.VMEM((N, 2, 2, *block), BF16),
            dma((N,)), dma((N,)),
            dma((N,)), dma((N,)),
            dma((N,)), dma((N,)),
            dma, dma,
            dma((N,)), dma((N,)),
            dma((N,)), dma,
            dma((N,)), dma((N,)),
            dma((N, CHIPS)), dma((N, CHIPS)),
            dma((N,)), dma((N,)),
        ],
        compiler_params=pltpu.CompilerParams(
            collective_id=0, has_side_effects=True, vmem_limit_bytes=40 << 20
        ),
        name="exchange",
    )(cb, live, fin, contrib, fct)


def update_kernel(cb, live, fin, xr, t, pc, out, total, strip, rowq, colq, colc, jof, sem):
    row = lax.axis_index("row")
    col = lax.axis_index("col")

    def strip_copy(p):
        rows = pl.ds(pl.multiple_of(p * BLK, BLK), BLK)
        return pltpu.make_async_copy(strip.at[p % 2], out.at[rows], sem.at[p % 2])

    @pl.when(row >= col)
    def _():
        for i in range(4 * N):
            rowq[i] = -1
            colq[i] = -1
        for j in range(N):
            jof[fin[j]] = j
        for c in range(4):
            for q in range(BLOCKS):
                v = cb[c, q]
                m = 4 * (q % 3) + (q // 3) % 4
                before = q - q % 12 + 3 * ((m - 1) % 4) + (m - 1) // 4

                @pl.when(v >> 3 == row)
                def _():
                    rowq[N * c + (v & 7)] = q

                @pl.when(v >> 3 == col)
                def _():
                    colq[N * c + (v & 7)] = q
                    if m == 0:
                        colc[N * c + (v & 7)] = 0
                    else:
                        colc[N * c + (v & 7)] = jnp.where(cb[c, before] >> 3 == col, 1, 0)

    def one_strip(p):
        rows = t[p]
        for b in range(0, N, 2):
            columns = pc[b : b + 2].reshape(2 * BLK, PANEL)
            total[:, b * BLK : (b + 2) * BLK] = -lax.dot_general(
                rows, columns, (((1,), (1,)), ((), ())), preferred_element_type=F32
            )
        for c in range(4):
            q = rowq[N * c + p]

            @pl.when((q >= 0) & (q < live[c]))
            def _():
                r = q // 3
                for b in range(N):
                    s = colq[N * c + b]

                    @pl.when((s >= 0) & (s <= q))
                    def _():
                        j = jof[2 * c + jnp.where(s >= 12, 1, 0)]
                        block = xr[r % 2, j, r // 2, colc[N * c + b]]
                        total[:, b * BLK : (b + 1) * BLK] += block.astype(F32)

        ri = (N * row + p) * BLK + lax.broadcasted_iota(jnp.int32, (BLK, N * BLK), 0)
        ci = N * BLK * col + lax.broadcasted_iota(jnp.int32, (BLK, N * BLK), 1)
        keep = (ri >= ci) & (ri >= PANEL) & (ci >= PANEL)
        strip[p % 2] = jnp.where(keep, total[...], 0.0).astype(BF16)

    @pl.when(row < col)
    def _():
        strip[...] = jnp.zeros_like(strip)

    @pl.loop(0, N)
    def _(p):
        @pl.when(p >= 2)
        def _():
            strip_copy(p - 2).wait()

        @pl.when(row >= col)
        def _():
            one_strip(p)

        strip_copy(p).start()

    for p in range(N - 2, N):
        strip_copy(p).wait()


def update(cb, live, fin, xr, t, pc):
    smem = pl.BlockSpec(memory_space=pltpu.SMEM)
    vmem = pl.BlockSpec(memory_space=pltpu.VMEM)
    ints = lambda n: pltpu.SMEM((n,), jnp.int32)
    return pl.pallas_call(
        update_kernel,
        out_shape=jax.ShapeDtypeStruct((N * BLK, N * BLK), BF16),
        in_specs=[smem] * 3 + [vmem] * 3,
        out_specs=pl.BlockSpec(memory_space=pl.ANY),
        scratch_shapes=[
            pltpu.VMEM((BLK, N * BLK), F32),
            pltpu.VMEM((2, BLK, N * BLK), BF16),
            ints(4 * N), ints(4 * N), ints(4 * N), ints(N),
            pltpu.SemaphoreType.DMA((2,)),
        ],
        compiler_params=pltpu.CompilerParams(vmem_limit_bytes=40 << 20),
        name="update",
    )(cb, live, fin, xr, t, pc)


def body(front_cols, contrib, child_blocks, child_live, finish):
    pieces = contrib.reshape(3, BLK, 12 * BLK)
    xr, t, pc = exchange(child_blocks, child_live, finish, pieces, front_cols.T)
    return update(child_blocks, child_live, finish, xr, t, pc)


def solution(mesh):
    return jax.shard_map(
        body,
        mesh=mesh,
        in_specs=(
            P(("front", "row"), "col"),
            P(("front", "col"), "row", None),
            P("front", None),
            P("front"),
            P("front"),
        ),
        out_specs=P(("front", "row"), "col"),
        check_vma=False,
    )
```

```python
import jax
import jax.numpy as jnp
from jax import lax
from jax.experimental import pallas as pl
from jax.experimental.pallas import tpu as pltpu
from jax.sharding import PartitionSpec as P

BLK = 128
PANEL = 256
N = 8
CHIPS = 4
BLOCKS = 24
BF16 = jnp.bfloat16
F32 = jnp.float32
LAG = 3
EARLY = 3
BEFORE_SUM = 5
SUM_STEP = 3
COLUMNS_STEP = 5
FIRST_BLOCK = 4
RING_STEP = 5


def copy_to(src, dst, send, recv, **device):
    return pltpu.make_async_remote_copy(
        src_ref=src,
        dst_ref=dst,
        send_sem=send,
        recv_sem=recv,
        device_id=device,
        device_id_type=pl.DeviceIdType.MESH,
    )


def ring_offset(i):
    return jnp.where(i % 2 == 1, (i + 1) // 2, (N - i // 2) % N)


def first_kept(row, col):
    return jnp.maximum(col - 1 - (row % 4) // 2, 0) // 2


def chosen(cases):
    value = cases[0][1]
    for holds, other in cases[1:]:
        value = jnp.where(holds, other, value)
    return value


def column_block(m):
    place = 3 * (m % 4) + m // 4
    return slice(place * BLK, (place + 1) * BLK)


def dot(a, b):
    ah = a.astype(BF16)
    bh = b.astype(BF16)
    al = (a - ah.astype(F32)).astype(BF16)
    bl = (b - bh.astype(F32)).astype(BF16)
    return product(ah, bh) + (product(ah, bl) + product(al, bh))


def product(a, b):
    return jnp.dot(a, b, preferred_element_type=F32)


STEP = 32
TOGETHER = 8


def small_inverse(d):
    n = d.shape[0]
    rows = lax.broadcasted_iota(jnp.int32, (n, n), 0)
    cols = lax.broadcasted_iota(jnp.int32, (n, n), 1)
    for k in range(0, n, TOGETHER):
        down = [jnp.broadcast_to(d[:, k + i : k + i + 1], (n, n)) for i in range(TOGETHER)]
        across = [d[k + i : k + i + 1, :] for i in range(TOGETHER)]
        for p in range(TOGETHER):
            at = k + p
            base = down[p]
            inv = 1.0 / base[at : at + 1, :]
            scales = [base[k + i : k + i + 1, :] * inv for i in range(TOGETHER)]
            scaled = across[p] * inv
            d = d - base * scaled
            for i in range(TOGETHER):
                if i != p:
                    down[i] = jnp.where(rows == at, scales[i], down[i] - base * scales[i])
                    across[i] = across[i] - scales[i] * across[p]
            down[p] = jnp.where(rows == at, -inv, base * inv)
            across[p] = scaled
        for i in range(TOGETHER):
            d = jnp.where(rows == k + i, across[i], d)
        for i in range(TOGETHER):
            d = jnp.where(cols == k + i, down[i], d)
    return -d


def sweep_block(a):
    across = a[0:STEP, :]
    down = a[:, 0:STEP]
    inv = small_inverse(a[0:STEP, 0:STEP])
    q = dot(inv, across)
    qt = dot(down, inv)
    a[...] = a[...] - dot(qt, across)
    a[0:STEP, :] = q
    a[:, 0:STEP] = qt
    a[0:STEP, 0:STEP] = -inv
    n = a.shape[0]
    a[...] = pltpu.roll(pltpu.roll(a[...], n - STEP, 0), n - STEP, 1)


def from_lower(a, co):
    lower = jnp.concatenate([co[0], co[1]], axis=0).astype(F32)
    ri = lax.broadcasted_iota(jnp.int32, (PANEL, PANEL), 0)
    ci = lax.broadcasted_iota(jnp.int32, (PANEL, PANEL), 1)
    a[...] = lower + jnp.where(ri < ci, lower.T, 0.0)


def times_inverse(t, pr, a):
    m = -a[...]
    high = m.astype(BF16)
    low = (m - high.astype(F32)).astype(BF16)
    for b in range(0, N, 2):
        rows = pr[b : b + 2].reshape(2 * BLK, PANEL)
        both = product(rows, high) + product(rows, low)
        t[b : b + 2] = both.astype(BF16).reshape(2, BLK, PANEL)


def exchange_kernel(
    cb, live, fin, contrib, fct,
    xr, t, pc,
    a, px, pxr, pz, pzr, pb, pr, pt, co, zs, zr, xs,
    px_s, px_r, pz_s, pz_r, pr_s, pr_r, t_s, t_r, pc_s, pc_r, co_s, co_r,
    z_s, z_r, x_s, x_r, f_s, f_r,
):
    row = lax.axis_index("row")
    col = lax.axis_index("col")
    chip = row // 2
    core = row % 2
    mate = 2 * chip + 1 - core

    barrier = pltpu.get_barrier_semaphore()

    @pl.loop(1, N)
    def _(d):
        pl.semaphore_signal(barrier, 1, device_id={"row": (row + d) % N}, device_id_type=pl.DeviceIdType.MESH)
        pl.semaphore_signal(barrier, 1, device_id={"col": (col + d) % N}, device_id_type=pl.DeviceIdType.MESH)

    @pl.when(row != col)
    def _():
        pl.semaphore_signal(barrier, 1, device_id={"row": col, "col": row}, device_id_type=pl.DeviceIdType.MESH)

    piece = fin[col]
    child = piece >> 1
    half = piece & 1
    groups = [cb[child, 3 * row + k] >> 3 for k in range(3)]
    for dest in range(N):
        px[dest] = chosen([(groups[k] == dest, contrib[k, :, 0:BLK]) for k in range(3)])
    pxr[row] = px[row]

    @pl.when(row == col)
    def _():
        pl.semaphore_wait(barrier, 2 * N - 2)

    @pl.when(row != col)
    def _():
        pl.semaphore_wait(barrier, 2 * N - 1)

    def px_copy(dest, slot):
        return copy_to(px.at[dest], pxr.at[slot], px_s.at[dest], px_r.at[slot], row=dest)

    @pl.loop(1, N)
    def _(d):
        dest = (row + d) % N
        px_copy(dest, row).start()

    col_groups = [cb[child, 12 * half + 3 * (m % 4) + m // 4] >> 3 for m in range(12)]
    for dest in range(N):
        first = sum(jnp.where(g < dest, 1, 0) for g in col_groups)
        for k in range(0 if dest < 4 else 1 if dest < 6 else 2, 3):
            for c in range(2):
                ms = range(max(0, 2 * dest - 4 + c), min(2 * dest + 1, 4 * k + 3) + 1)
                zs[dest, k, c] = chosen([(first == m - c, contrib[k, :, column_block(m)]) for m in ms])
    zr[col] = zs[col]

    def z_copies(dest, slot, by, act):
        for k in range(3):
            @pl.when(first_kept(row, by) == k)
            def _():
                act(copy_to(
                    zs.at[dest, pl.ds(k, 3 - k)], zr.at[slot, pl.ds(k, 3 - k)],
                    z_s.at[dest], z_r.at[slot], col=dest,
                ))

    def start_z(first, end):
        @pl.loop(first, end)
        def _(i):
            dest = (col + ring_offset(i)) % N
            z_copies(dest, col, dest, lambda copy: copy.start())

    start_z(1, EARLY)

    from_row = [jnp.int32(0)] * N
    for q in range(BLOCKS):
        at = cb[child, q] - N * row
        from_row = [jnp.where(at == b, q // 3, from_row[b]) for b in range(N)]

    @pl.loop(1, N)
    def _(d):
        px_copy((row + d) % N, (row + d) % N).wait_recv()

    for b in range(N):
        pz[b, 0:BLK] = chosen([(from_row[b] == r, pxr[r]) for r in range(N)])
        pz[b, BLK:] = fct[:, b * BLK : (b + 1) * BLK]
    pzr[col] = pz[col]

    def pz_copy(dest, slot):
        return copy_to(pz.at[dest], pzr.at[slot], pz_s.at[dest], pz_r.at[slot], col=dest)

    @pl.loop(0, N)
    def _(i):
        dest = jnp.where(row == 0, i, (col + ring_offset(i)) % N)

        @pl.when(dest != col)
        def _():
            pz_copy(dest, col).start()

    start_z(EARLY, BEFORE_SUM)

    def pr_copy(dest, slot):
        return copy_to(pb, pr.at[slot], pr_s.at[dest], pr_r.at[slot], col=dest)

    pt_copy = copy_to(pb, pt, t_s, t_r, row=col, col=row)

    def co_copy(dest):
        return copy_to(pr.at[pl.ds(0, 2)], co, co_s.at[dest], co_r, row=dest)

    def ring_copy(s, right):
        if right:
            block, dest = (col + N - s) % N, (col + 1) % N
        else:
            block, dest = (col + s) % N, (col + N - 1) % N
        sem = pr_s.at[s if right else 4 + s]
        return copy_to(pr.at[block], pr.at[block], sem, pr_r.at[block], col=dest)

    def ring_step(s):
        for right in (True, False):
            if s > 0:
                ring_copy(s, right).wait_recv()
            if right or s < 3:
                ring_copy(s, right).start()

    def sum_panel():
        @pl.loop(1, N)
        def _(i):
            pz_copy((col + i) % N, (col + i) % N).wait_recv()

        left = jnp.zeros((BLK, BLK), F32)
        right = jnp.zeros((BLK, BLK), F32)
        for j in range(N):
            c = fin[j] >> 1
            column = 12 * (fin[j] & 1)
            q = jnp.int32(-1)
            for entry in range(BLOCKS):
                q = jnp.where(cb[c, entry] == N * row + col, entry, q)
            at = cb[c, column]
            valid = (q >= column) & (q < live[c])
            block = pzr[j, 0:BLK].astype(F32)
            left += jnp.where(valid & (at == 0), block, 0.0)
            right += jnp.where(valid & (at == 1), block, 0.0)
        initial = jnp.concatenate([pzr[j, BLK:] for j in range(N)], axis=0).astype(F32).T
        row_ids = (N * row + col) * BLK + lax.broadcasted_iota(jnp.int32, (BLK, PANEL), 0)
        col_ids = lax.broadcasted_iota(jnp.int32, (BLK, PANEL), 1)
        total = jnp.concatenate([left, right], axis=1) + initial
        pb[...] = jnp.where(row_ids >= col_ids, total, 0.0).astype(BF16)
        pr[col] = pb[...]

        @pl.when(row == 0)
        def _():
            @pl.loop(1, N)
            def _(i):
                dest = (col + ring_offset(i)) % N

                @pl.when((dest == 0) | (col < 2))
                def _():
                    pr_copy(dest, col).start()

        @pl.when(row > 0)
        def _():
            ring_step(0)

        @pl.when(row != col)
        def _():
            pt_copy.start()

        @pl.when(row == col)
        def _():
            pt[...] = pb[...]

        start_z(BEFORE_SUM, N)

        @pl.when(row == 0)
        def _():
            for b in range(2):
                @pl.when(col != b)
                def _():
                    pr_copy(b, b).wait_recv()

            @pl.loop(1, N)
            def _(dest):
                co_copy(dest).start()

            co[...] = pr[0:2]

    def pc_copy(dest, slot):
        return copy_to(pt, pc.at[slot], pc_s.at[dest], pc_r.at[slot], row=dest)

    def pass_on_columns():
        @pl.when(row != col)
        def _():
            pt_copy.wait_recv()

        @pl.loop(1, N)
        def _(i):
            dest = (row + i) % N

            @pl.when(dest >= col)
            def _():
                pc_copy(dest, row).start()

        pc[row] = pt[...]

    needed = chip >= col // 2

    def x_copy(j, src, dest, slot):
        return copy_to(src, xr.at[core, j, slot], x_s.at[j, dest], x_r.at[j, slot], row=2 * dest + core)

    def f_copy(j, side):
        return copy_to(xr.at[side, j], xr.at[side, j], f_s.at[j], f_r.at[j], row=mate)

    @pl.loop(0, N + LAG)
    def _(i):
        j = (col + ring_offset(i)) % N

        @pl.when(i < N)
        def _():
            @pl.when(i == SUM_STEP)
            def _():
                sum_panel()

            @pl.when(i == COLUMNS_STEP)
            def _():
                pass_on_columns()

            for s in range(1, 4):
                @pl.when((i == RING_STEP + s - 1) & (row > 0))
                def _():
                    ring_step(s)

            @pl.when(i > 0)
            def _():
                z_copies(j, j, col, lambda copy: copy.wait_recv())

            c = fin[j] >> 1
            for dest in range(CHIPS):
                @pl.when(2 * dest + 1 >= col)
                def _():
                    if dest == 0:
                        src = zr.at[j, 0]
                    elif dest == 3:
                        src = zr.at[j, 2]
                    else:
                        src = xs.at[j, dest - 1]
                        later = (cb[c, 3 * row + dest] >> 4) == dest
                        src[...] = jnp.where(later, zr[j, dest], zr[j, dest - 1])

                    @pl.when(chip == dest)
                    def _():
                        xr[core, j, chip] = src[...]

                    @pl.when(chip != dest)
                    def _():
                        x_copy(j, src, dest, chip).start()

        @pl.when((i >= LAG) & needed)
        def _():
            before = (col + ring_offset(i - LAG)) % N
            for slot in range(CHIPS):
                @pl.when(chip != slot)
                def _():
                    x_copy(before, xs.at[before, 0], slot, slot).wait_recv()

            f_copy(before, core).start()

        @pl.when(i == FIRST_BLOCK)
        def _():
            @pl.when(row != 0)
            def _():
                co_copy(row).wait_recv()

            from_lower(a, co)

        @pl.when((i >= FIRST_BLOCK) & (i < FIRST_BLOCK + 4) & (row >= col))
        def _():
            @pl.loop(0, 2)
            def _(_i):
                sweep_block(a)

    @pl.when(row > 0)
    def _():
        last = (col + 4) % N
        pr_copy(last, last).wait_recv()

    @pl.when((row == 0) & (col == 0))
    def _():
        @pl.loop(2, N)
        def _(b):
            pr_copy(b, b).wait_recv()

    @pl.when(row >= col)
    def _():
        times_inverse(t, pr, a)

        @pl.loop(1, N)
        def _(i):
            slot = (row + i) % N
            pc_copy(slot, slot).wait_recv()

    @pl.when(needed)
    def _():
        @pl.loop(0, N)
        def _(j):
            f_copy(j, 1 - core).wait_recv()

    @pl.loop(1, N)
    def _(i):
        r = (row + i) % N
        c = (col + i) % N
        px_copy(r, row).wait_send()
        pz_copy(c, col).wait_send()
        z_copies(c, col, c, lambda copy: copy.wait_send())

        @pl.when((row == 0) & ((c == 0) | (col < 2)))
        def _():
            pr_copy(c, col).wait_send()

        @pl.when(r >= col)
        def _():
            pc_copy(r, row).wait_send()

        @pl.when(row == 0)
        def _():
            co_copy(r).wait_send()

    @pl.when(row > 0)
    def _():
        for s in range(4):
            ring_copy(s, True).wait_send()
            if s < 3:
                ring_copy(s, False).wait_send()

    @pl.when(row != col)
    def _():
        pt_copy.wait_send()

    @pl.loop(0, N)
    def _(j):
        for dest in range(CHIPS):
            @pl.when((2 * dest + 1 >= col) & (chip != dest))
            def _():
                x_copy(j, xs.at[j, 0], dest, chip).wait_send()

        @pl.when(needed)
        def _():
            f_copy(j, core).wait_send()


def exchange(cb, live, fin, contrib, fct):
    dma = pltpu.SemaphoreType.DMA
    vmem = pl.BlockSpec(memory_space=pltpu.VMEM)
    smem = pl.BlockSpec(memory_space=pltpu.SMEM)
    block = (BLK, BLK)
    panel = (BLK, PANEL)
    return pl.pallas_call(
        exchange_kernel,
        out_shape=[
            jax.ShapeDtypeStruct((2, N, CHIPS, 2, *block), BF16),
            jax.ShapeDtypeStruct((N, *panel), BF16),
            jax.ShapeDtypeStruct((N, *panel), BF16),
        ],
        in_specs=[smem, smem, smem, vmem, vmem],
        out_specs=[vmem] * 3,
        scratch_shapes=[
            pltpu.VMEM((PANEL, PANEL), F32),
            pltpu.VMEM((N, *block), BF16),
            pltpu.VMEM((N, *block), BF16),
            pltpu.VMEM((N, BLK + 32, BLK), BF16),
            pltpu.VMEM((N, BLK + 32, BLK), BF16),
            pltpu.VMEM(panel, BF16),
            pltpu.VMEM((N, *panel), BF16),
            pltpu.VMEM(panel, BF16),
            pltpu.VMEM((2, *panel), BF16),
            pltpu.VMEM((N, 3, 2, *block), BF16),
            pltpu.VMEM((N, 3, 2, *block), BF16),
            pltpu.VMEM((N, 2, 2, *block), BF16),
            dma((N,)), dma((N,)),
            dma((N,)), dma((N,)),
            dma((N,)), dma((N,)),
            dma, dma,
            dma((N,)), dma((N,)),
            dma((N,)), dma,
            dma((N,)), dma((N,)),
            dma((N, CHIPS)), dma((N, CHIPS)),
            dma((N,)), dma((N,)),
        ],
        compiler_params=pltpu.CompilerParams(
            collective_id=0, has_side_effects=True, vmem_limit_bytes=40 << 20
        ),
        name="exchange",
    )(cb, live, fin, contrib, fct)


def update_kernel(cb, live, fin, xr, t, pc, out, total, strip, rowq, colq, colc, jof, sem):
    row = lax.axis_index("row")
    col = lax.axis_index("col")

    def strip_copy(p):
        rows = pl.ds(pl.multiple_of(p * BLK, BLK), BLK)
        return pltpu.make_async_copy(strip.at[p % 2], out.at[rows], sem.at[p % 2])

    @pl.when(row >= col)
    def _():
        for i in range(4 * N):
            rowq[i] = -1
            colq[i] = -1
        for j in range(N):
            jof[fin[j]] = j
        for c in range(4):
            for q in range(BLOCKS):
                v = cb[c, q]
                m = 4 * (q % 3) + (q // 3) % 4
                before = q - q % 12 + 3 * ((m - 1) % 4) + (m - 1) // 4

                @pl.when(v >> 3 == row)
                def _():
                    rowq[N * c + (v & 7)] = q

                @pl.when(v >> 3 == col)
                def _():
                    colq[N * c + (v & 7)] = q
                    if m == 0:
                        colc[N * c + (v & 7)] = 0
                    else:
                        colc[N * c + (v & 7)] = jnp.where(cb[c, before] >> 3 == col, 1, 0)

    def one_strip(p):
        rows = t[p]
        for b in range(0, N, 2):
            columns = pc[b : b + 2].reshape(2 * BLK, PANEL)
            total[:, b * BLK : (b + 2) * BLK] = -lax.dot_general(
                rows, columns, (((1,), (1,)), ((), ())), preferred_element_type=F32
            )
        for c in range(4):
            q = rowq[N * c + p]

            @pl.when((q >= 0) & (q < live[c]))
            def _():
                r = q // 3
                for b in range(N):
                    s = colq[N * c + b]

                    @pl.when((s >= 0) & (s <= q))
                    def _():
                        j = jof[2 * c + jnp.where(s >= 12, 1, 0)]
                        block = xr[r % 2, j, r // 2, colc[N * c + b]]
                        total[:, b * BLK : (b + 1) * BLK] += block.astype(F32)

        ri = (N * row + p) * BLK + lax.broadcasted_iota(jnp.int32, (BLK, N * BLK), 0)
        ci = N * BLK * col + lax.broadcasted_iota(jnp.int32, (BLK, N * BLK), 1)
        keep = (ri >= ci) & (ri >= PANEL) & (ci >= PANEL)
        strip[p % 2] = jnp.where(keep, total[...], 0.0).astype(BF16)

    @pl.when(row < col)
    def _():
        strip[...] = jnp.zeros_like(strip)

    @pl.loop(0, N)
    def _(p):
        @pl.when(p >= 2)
        def _():
            strip_copy(p - 2).wait()

        @pl.when(row >= col)
        def _():
            one_strip(p)

        strip_copy(p).start()

    for p in range(N - 2, N):
        strip_copy(p).wait()


def update(cb, live, fin, xr, t, pc):
    smem = pl.BlockSpec(memory_space=pltpu.SMEM)
    vmem = pl.BlockSpec(memory_space=pltpu.VMEM)
    ints = lambda n: pltpu.SMEM((n,), jnp.int32)
    return pl.pallas_call(
        update_kernel,
        out_shape=jax.ShapeDtypeStruct((N * BLK, N * BLK), BF16),
        in_specs=[smem] * 3 + [vmem] * 3,
        out_specs=pl.BlockSpec(memory_space=pl.ANY),
        scratch_shapes=[
            pltpu.VMEM((BLK, N * BLK), F32),
            pltpu.VMEM((2, BLK, N * BLK), BF16),
            ints(4 * N), ints(4 * N), ints(4 * N), ints(N),
            pltpu.SemaphoreType.DMA((2,)),
        ],
        compiler_params=pltpu.CompilerParams(vmem_limit_bytes=40 << 20),
        name="update",
    )(cb, live, fin, xr, t, pc)


def body(front_cols, contrib, child_blocks, child_live, finish):
    pieces = contrib.reshape(3, BLK, 12 * BLK)
    xr, t, pc = exchange(child_blocks, child_live, finish, pieces, front_cols.T)
    return update(child_blocks, child_live, finish, xr, t, pc)


def solution(mesh):
    return jax.shard_map(
        body,
        mesh=mesh,
        in_specs=(
            P(("front", "row"), "col"),
            P(("front", "col"), "row", None),
            P("front", None),
            P("front"),
            P("front"),
        ),
        out_specs=P(("front", "row"), "col"),
        check_vma=False,
    )
```
